256 devices in a mesh: seq: 128 (over y, z_lo, x, core), batch: 2 (over z_hi).
Axes of the slice: x: 4, y: 4, z: 8 (z_hi: 2, z_lo: 4; z = z_hi * 4 + z_lo), core: 2. Of those that a mesh axis runs over, the one named last changes fastest.
Arguments:
- queries: bfloat16 [2, 16384, 2048], P('batch', 'seq'), may hold values from -8 to 8
- key_rows: bfloat16 [2, 16384, 2048], P('batch', 'seq'), may hold values from -8 to 8
- values: bfloat16 [2, 16384, 2048], P('batch', 'seq'), may hold values from -6 to 6
- cotangent: bfloat16 [2, 16384, 2048], P('batch', 'seq'), may hold values from -6 to 6
- level_bias: float32 [3, 16], replicated, may hold values from -1 to 1
Outputs:
- attended: bfloat16 [2, 16384, 2048], P('batch', 'seq')
- query_grad: bfloat16 [2, 16384, 2048], P('batch', 'seq')
- key_grad: bfloat16 [2, 16384, 2048], P('batch', 'seq')
- value_grad: bfloat16 [2, 16384, 2048], P('batch', 'seq')
- level_grad: float32 [3, 16], replicated
The draws below stay inside these ranges and needn't reach their ends.
All inputs are finite; a program needn't handle non-finite values.
Results may differ from the reference program's by a relative error of at most 0.0025.
The reference program's roundings to bfloat16 on the way (of `level_keys_1`, `level_keys_2`, `weights_low` and `score_low`) count: a program that leaves them out, or rounds other values in their place, can miss the bound.
Values may be sent and summed in bfloat16 or wider, within the bound.
No kernel may reach another device: no remote copies, remote signals or barrier semaphores. Data moves between devices by JAX's collectives and lax.ppermute only.
A program may use at most 128 MiB of HBM per device.

```python
import math
import jax
import jax.numpy as jnp
from jax import lax

HEADS = 16
D = 2048
TOK_DEV = 128
BATCH = 2
POOL1 = 16
POOL2 = 128
GROUP = 16
SEQ = 16384
N_SEQ = 128


def draw_queries(key, part):
    key = jax.random.fold_in(key, 11)
    drawn = jnp.clip(1.5 * jax.random.normal(key, (BATCH, SEQ, D), jnp.float32), -8.0, 8.0)
    return drawn.astype(jnp.bfloat16)


def draw_key_rows(key, part):
    key = jax.random.fold_in(key, 23)
    drawn = jnp.clip(1.5 * jax.random.normal(key, (BATCH, SEQ, D), jnp.float32), -8.0, 8.0)
    return drawn.astype(jnp.bfloat16)


def steps_of(stream_key, extent, split, smallest, top_value):
    loudness, own = 1.0, jax.random.fold_in(stream_key, 6)
    for dim, blocks in split:
        heights = jnp.exp(jax.random.uniform(jax.random.fold_in(own, dim), (blocks,), jnp.float32, smallest / len(split), top_value / len(split)))
        loudness = loudness * jnp.repeat(heights, extent[dim] // blocks).reshape([-1 if axis == dim else 1 for axis in range(len(extent))])
    return loudness


def centred(own_key, extent, deviation, most, cuts=(), kind=jnp.bfloat16):
    result = deviation * jax.random.normal(own_key, extent, jnp.float32)
    if cuts:
        result = result * steps_of(own_key, extent, cuts, -0.22, 0.18)
    return jnp.clip(result, -most, most).astype(kind)


def setup_inputs(seed: int = 0) -> dict:
    keys = jax.random.split(jax.random.key(seed), 6)
    return {
        "queries": draw_queries(jax.random.fold_in(keys[5], 71), 0),
        "key_rows": draw_key_rows(jax.random.fold_in(keys[5], 71), 0),
        "values": centred(keys[2], (BATCH, SEQ, D), 1.0, 6.0, ((0, 2), (1, 128))),
        "cotangent": centred(keys[3], (BATCH, SEQ, D), 1.0, 6.0, ((0, 2), (1, 128))),
        "level_bias": jnp.clip(jax.random.uniform(keys[4], (3, HEADS), jnp.float32, -1.0, 1.0), -1.0, 1.0),
    }


NEGATIVE = -1e30


def pooled(x, factor):
    b, n, d = x.shape
    return (jnp.sum(x.astype(jnp.float32).reshape(b, n // factor, factor, d), axis=2) / factor).astype(jnp.bfloat16)


def spread(x, factor):
    b, n, d = x.shape
    return jnp.broadcast_to((x / factor)[:, :, None, :], (b, n, factor, d)).reshape(b, n * factor, d)


def offsets(level_bias, fine_ok, group_ok, far_ok):
    fine_part = level_bias[0][:, None] + jnp.where(fine_ok, 0.0, NEGATIVE)[None, :]
    group_part = level_bias[1][:, None] + math.log(POOL1) + jnp.where(group_ok, 0.0, NEGATIVE)[None, :]
    far_part = level_bias[2][:, None] + math.log(POOL2) + jnp.where(far_ok, 0.0, NEGATIVE)[None, :]
    return jnp.concatenate([fine_part, group_part, far_part], axis=1)


def heads_of(x, head_count):
    b, n, d = x.shape
    return x.reshape(b, n, head_count, d // head_count)


def attend(query_rows, key_all, value_all, cotangent_rows, offset, fine_end, group_end):
    head_count = offset.shape[0]
    b, n, d = query_rows.shape
    score_scale = (d // head_count) ** -0.5
    head_queries = heads_of(query_rows.astype(jnp.float32), head_count)
    head_keys = heads_of(key_all.astype(jnp.float32), head_count)
    head_values = heads_of(value_all.astype(jnp.float32), head_count)
    head_cot = heads_of(cotangent_rows.astype(jnp.float32), head_count)
    scores = jnp.einsum('bthe,bkhe->bhtk', head_queries, head_keys) * score_scale + offset[None, :, None, :]
    row_top = jnp.max(scores, axis=-1, keepdims=True)
    log_total = row_top + jnp.log(jnp.sum(jnp.exp(scores - row_top), axis=-1, keepdims=True))
    weights = jnp.exp(scores - log_total)
    weights_low = lax.optimization_barrier(weights.astype(jnp.bfloat16)).astype(jnp.float32)
    attended = jnp.einsum('bhtk,bkhe->bthe', weights_low, head_values).reshape(b, n, d).astype(jnp.bfloat16)
    weight_grad = jnp.einsum('bthe,bkhe->bhtk', head_cot, head_values)
    row_delta = jnp.sum(weights * weight_grad, axis=-1, keepdims=True)
    score_grad = weights * (weight_grad - row_delta)
    score_low = lax.optimization_barrier(score_grad.astype(jnp.bfloat16)).astype(jnp.float32)
    query_grad = (jnp.einsum('bhtk,bkhe->bthe', score_low, head_keys) * score_scale).reshape(b, n, d).astype(jnp.bfloat16)
    key_grad = (jnp.einsum('bhtk,bthe->bkhe', score_low, head_queries) * score_scale).reshape(b, -1, d)
    value_grad = jnp.einsum('bhtk,bthe->bkhe', weights_low, head_cot).reshape(b, -1, d)
    level_terms = jnp.stack([
        jnp.sum(score_grad[..., :fine_end], axis=(0, 2, 3)),
        jnp.sum(score_grad[..., fine_end:group_end], axis=(0, 2, 3)),
        jnp.sum(score_grad[..., group_end:], axis=(0, 2, 3))])
    return attended, query_grad, key_grad, value_grad, level_terms


def reference(queries, key_rows, values, cotangent, level_bias):
    b, total, d = queries.shape
    group_rows = TOK_DEV // POOL1
    far_rows = TOK_DEV // POOL2
    fine_end = 3 * TOK_DEV
    group_end = fine_end + GROUP * group_rows
    level_keys_1 = pooled(key_rows, POOL1)
    level_values_1 = pooled(values, POOL1)
    level_keys_2 = pooled(key_rows, POOL2)
    level_values_2 = pooled(values, POOL2)
    padding = ((0, 0), (TOK_DEV, TOK_DEV), (0, 0))
    padded_keys = jnp.pad(key_rows, padding)
    padded_values = jnp.pad(values, padding)
    fine_columns = jnp.arange(3 * TOK_DEV, dtype=jnp.int32) // TOK_DEV
    group_columns = jnp.arange(GROUP * group_rows, dtype=jnp.int32) // group_rows
    far_columns = jnp.arange(N_SEQ * far_rows, dtype=jnp.int32) // far_rows

    def block_step(carry, block_index):
        fine_keys, fine_values, group_keys, group_values, far_keys, far_values, level_sum = carry
        first_row = block_index * TOK_DEV
        group_first = (block_index // GROUP) * (GROUP * group_rows)
        query_rows = lax.dynamic_slice_in_dim(queries, first_row, TOK_DEV, 1)
        cotangent_rows = lax.dynamic_slice_in_dim(cotangent, first_row, TOK_DEV, 1)
        near_keys = lax.dynamic_slice_in_dim(padded_keys, first_row, fine_end, 1)
        near_values = lax.dynamic_slice_in_dim(padded_values, first_row, fine_end, 1)
        member_keys = lax.dynamic_slice_in_dim(level_keys_1, group_first, GROUP * group_rows, 1)
        member_values = lax.dynamic_slice_in_dim(level_values_1, group_first, GROUP * group_rows, 1)
        fine_owner = block_index - 1 + fine_columns
        fine_ok = (fine_owner >= 0) & (fine_owner < N_SEQ)
        group_owner = (block_index // GROUP) * GROUP + group_columns
        group_ok = jnp.abs(group_owner - block_index) >= 2
        far_ok = (far_columns // GROUP != block_index // GROUP) & (jnp.abs(far_columns - block_index) >= 2)
        offset = offsets(level_bias, fine_ok, group_ok, far_ok)
        key_all = jnp.concatenate([near_keys, member_keys, level_keys_2], axis=1)
        value_all = jnp.concatenate([near_values, member_values, level_values_2], axis=1)
        attended, query_grad, key_grad, value_grad, level_terms = attend(
            query_rows, key_all, value_all, cotangent_rows, offset, fine_end, group_end)
        fine_keys = lax.dynamic_update_slice_in_dim(
            fine_keys, lax.dynamic_slice_in_dim(fine_keys, first_row, fine_end, 1) + key_grad[:, :fine_end], first_row, 1)
        fine_values = lax.dynamic_update_slice_in_dim(
            fine_values, lax.dynamic_slice_in_dim(fine_values, first_row, fine_end, 1) + value_grad[:, :fine_end], first_row, 1)
        group_keys = lax.dynamic_update_slice_in_dim(
            group_keys, lax.dynamic_slice_in_dim(group_keys, group_first, GROUP * group_rows, 1) + key_grad[:, fine_end:group_end], group_first, 1)
        group_values = lax.dynamic_update_slice_in_dim(
            group_values, lax.dynamic_slice_in_dim(group_values, group_first, GROUP * group_rows, 1) + value_grad[:, fine_end:group_end], group_first, 1)
        far_keys = far_keys + key_grad[:, group_end:]
        far_values = far_values + value_grad[:, group_end:]
        level_sum = level_sum + level_terms
        return (fine_keys, fine_values, group_keys, group_values, far_keys, far_values, level_sum), (attended, query_grad)

    init = (jnp.zeros((b, total + 2 * TOK_DEV, d), jnp.float32), jnp.zeros((b, total + 2 * TOK_DEV, d), jnp.float32),
            jnp.zeros((b, total // POOL1, d), jnp.float32), jnp.zeros((b, total // POOL1, d), jnp.float32),
            jnp.zeros((b, total // POOL2, d), jnp.float32), jnp.zeros((b, total // POOL2, d), jnp.float32),
            jnp.zeros((3, level_bias.shape[1]), jnp.float32))
    carry, (attended_blocks, query_blocks) = lax.scan(block_step, init, jnp.arange(N_SEQ, dtype=jnp.int32))
    fine_keys, fine_values, group_keys, group_values, far_keys, far_values, level_sum = carry
    attended = jnp.transpose(attended_blocks, (1, 0, 2, 3)).reshape(b, total, d)
    query_grad = jnp.transpose(query_blocks, (1, 0, 2, 3)).reshape(b, total, d)
    key_grad = (fine_keys[:, TOK_DEV:TOK_DEV + total] + spread(group_keys, POOL1) + spread(far_keys, POOL2)).astype(jnp.bfloat16)
    value_grad = (fine_values[:, TOK_DEV:TOK_DEV + total] + spread(group_values, POOL1) + spread(far_values, POOL2)).astype(jnp.bfloat16)
    return (attended, query_grad, key_grad, value_grad, level_sum)
```

```python
import functools
import math

import jax
import jax.numpy as jnp
from jax import lax
from jax.experimental import pallas as pl
from jax.experimental.pallas import tpu as pltpu
from jax.sharding import PartitionSpec as P

POOL1 = 16
POOL2 = 128
GROUP = 16
ROWS = 128
HEAD = 128
NEGATIVE = -1e30
LOG1 = math.log(POOL1)
LOG2 = math.log(POOL2)

SIB, Z1, YA, YB = 1, 16, 32, 96

BF = jnp.bfloat16
F32 = jnp.float32


def swap(x, mask):
    return lax.ppermute(x, "seq", [(i, i ^ mask) for i in range(lax.axis_size("seq"))])


def cross(x):
    size = lax.axis_size("seq")
    pairs = [(i, i + 1) for i in range(1, size - 1, 2)]
    return lax.ppermute(x, "seq", pairs + [(j, i) for i, j in pairs])


def in_group(x):
    size = lax.axis_size("seq")
    groups = [[g + i for i in range(GROUP)] for g in range(0, size, GROUP)]
    return lax.all_to_all(x, "seq", 0, 0, axis_index_groups=groups)


def params(limit=24):
    return pltpu.CompilerParams(vmem_limit_bytes=limit * 1024 * 1024)


def cost(us):
    return pl.CostEstimate(flops=0, bytes_accessed=int(us * 3.3e6), transcendentals=0)


def in_hbm(*arrays):
    return [pltpu.with_memory_space_constraint(x, pltpu.HBM) for x in arrays]


def out_hbm(shapes):
    return [pltpu.HBM(s.shape, s.dtype) for s in shapes]


def nt(a, b):
    return lax.dot_general(a, b, (((1,), (1,)), ((), ())), preferred_element_type=F32)


def nn(a, b):
    return lax.dot_general(a, b, (((1,), (0,)), ((), ())), preferred_element_type=F32)


def tn(a, b):
    return lax.dot_general(a, b, (((0,), (0,)), ((), ())), preferred_element_type=F32)


def pool_kernel(k_ref, v_ref, one_ref, two_ref):
    for n, ref in enumerate((k_ref, v_ref)):
        x = ref[...].astype(F32)
        sums = jnp.sum(x.reshape(ROWS // POOL1, POOL1, x.shape[-1]), axis=1)
        one_ref[8 * n : 8 * n + 8, :] = sums / POOL1
        row = jnp.sum(sums, axis=0, keepdims=True) / POOL2
        two_ref[0, n : n + 1, :] = row.astype(BF)


def pool(k, v):
    width = k.shape[1]
    return pl.pallas_call(
        pool_kernel,
        out_shape=(
            jax.ShapeDtypeStruct((16, width), F32),
            jax.ShapeDtypeStruct((1, 2, width), BF),
        ),
        compiler_params=params(),
        cost_estimate=cost(2),
    )(k, v)


def rows_kernel(one_ref, a_ref, b_ref, out_ref, far_ref):
    half = out_ref.shape[-1]
    for m, ref in enumerate((a_ref, b_ref)):
        for r in range(4):
            pair = ref[r].astype(F32)
            for n in range(2):
                to = 8 * n + 4 * m + r
                far_ref[to : to + 1, :] = pair[n : n + 1, :]
    for c in range(2):
        cols = slice(c * half, (c + 1) * half)
        one = one_ref[:, cols].astype(BF)
        far = far_ref[:, cols].astype(BF)
        for p in range(GROUP // 2):
            out_ref[2 * p + c, 0:16] = one
            out_ref[2 * p + c, 16:32] = far


def level_rows(one, a, b):
    width = one.shape[1]
    return pl.pallas_call(
        rows_kernel,
        out_shape=jax.ShapeDtypeStruct((GROUP, 32, width // 2), BF),
        scratch_shapes=[pltpu.VMEM((16, width), F32)],
        compiler_params=params(),
        cost_estimate=cost(1),
    )(one, a, b)


def prepare_kernel(ids_ref, *refs):
    arrays, wholes, halves, sems = refs[:4], refs[4:6], refs[6:10], refs[10]
    half = halves[0].shape[-1]
    start = pl.multiple_of((1 - ids_ref[1]) * half, half)
    copies = []
    for n, (ref, out) in enumerate(zip(arrays, halves)):
        to = wholes[n // 2].at[(n % 2) * ROWS : (n % 2 + 1) * ROWS]
        copies.append(pltpu.make_async_copy(ref, to, sems.at[2 * n]))
        part = ref.at[:, pl.ds(start, half)]
        copies.append(pltpu.make_async_copy(part, out, sems.at[2 * n + 1]))
    for copy in copies:
        copy.start()
    for copy in copies:
        copy.wait()


def prepare(ids, *arrays):
    rows, width = arrays[0].shape
    smem = pl.BlockSpec(memory_space=pltpu.SMEM)
    hbm = pl.BlockSpec(memory_space=pltpu.HBM)
    return pl.pallas_call(
        prepare_kernel,
        in_specs=[smem] + [hbm] * 4,
        out_specs=[hbm] * 6,
        out_shape=[jax.ShapeDtypeStruct((2 * rows, width), BF)] * 2
        + [jax.ShapeDtypeStruct((rows, width // 2), BF)] * 4,
        scratch_shapes=[pltpu.SemaphoreType.DMA((8,))],
        compiler_params=params(),
        cost_estimate=cost(1),
    )(ids, *arrays)


def other_kernel(ids_ref, x_ref, out_ref, sem):
    half = out_ref.shape[-1]
    start = pl.multiple_of((1 - ids_ref[1]) * half, half)
    part = x_ref.at[0 : out_ref.shape[0], pl.ds(start, half)]
    copy = pltpu.make_async_copy(part, out_ref, sem)
    copy.start()
    copy.wait()


def other_half(ids, x, rows):
    smem = pl.BlockSpec(memory_space=pltpu.SMEM)
    hbm = pl.BlockSpec(memory_space=pltpu.HBM)
    return pl.pallas_call(
        other_kernel,
        in_specs=[smem, hbm],
        out_specs=hbm,
        out_shape=jax.ShapeDtypeStruct((rows, x.shape[1] // 2), BF),
        scratch_shapes=[pltpu.SemaphoreType.DMA],
        compiler_params=params(),
        cost_estimate=cost(1),
    )(ids, x)


def split_rows(x):
    wide = x.astype(F32).reshape(GROUP, 16, HEAD)
    keys = wide[:, :8].reshape(ROWS, HEAD).astype(BF)
    return keys, wide[:, 8:].reshape(ROWS, HEAD).astype(BF)


def join_rows(a, b):
    both = [x.reshape(GROUP, 8, HEAD) for x in (a, b)]
    return jnp.concatenate(both, axis=1).astype(BF)


def pieces(sums):
    lane = lax.broadcasted_iota(jnp.int32, (1, HEAD), 1)
    row = jnp.zeros((1, HEAD), F32)
    for n, s in enumerate(sums):
        row = jnp.where(lane % 3 == n, jnp.sum(s, axis=1, keepdims=True), row)
    high = row.astype(BF).astype(F32)
    middle = (row - high).astype(BF).astype(F32)
    rest = row - high - middle
    row = jnp.where(lane < 3, high, jnp.where(lane < 6, middle, rest))
    return jnp.where(lane < 9, row, 0.0)


def attend_kernel(
    steps,
    heads,
    ids_ref,
    bias_ref,
    q_ref,
    k_ref,
    v_ref,
    c_ref,
    sq_ref,
    sk_ref,
    sv_ref,
    sc_ref,
    xk_ref,
    xv_ref,
    sxk_ref,
    sxv_ref,
    level_ref,
    att_ref,
    satt_ref,
    dq_ref,
    sdq_ref,
    dk_ref,
    dv_ref,
    sdk_ref,
    sdv_ref,
    glevel_ref,
    stat_ref,
    sstat_ref,
    mask_ref,
    edge_ref,
):
    step = pl.program_id(0)
    me, core = ids_ref[0], ids_ref[1]
    last = ids_ref[2] - 1
    scale = HEAD**-0.5

    @pl.when(step == 0)
    def _():
        row = lax.broadcasted_iota(jnp.int32, (ROWS, 2 * ROWS), 0)
        lane = lax.broadcasted_iota(jnp.int32, (ROWS, 2 * ROWS), 1)
        block = jnp.where(lane < ROWS, me, me ^ 1)
        group = me // GROUP
        place, which = row // 8, row % 8
        good = jnp.abs(group * GROUP + place - block) >= 2
        mask_ref[0:ROWS] = jnp.where(good, LOG1, NEGATIVE)
        owner = (group ^ (which ^ ((which >> 2) << 1))) * GROUP + place
        good = (which != 0) & (jnp.abs(owner - block) >= 2)
        mask_ref[ROWS:] = jnp.where(good, LOG2, NEGATIVE)
        lane = lane[0:8]
        block = block[0:8]
        edge_ref[...] = jnp.where((block == 0) | (block == last), NEGATIVE, 0.0)

    for j in range(heads):
        cols = slice(j * HEAD, (j + 1) * HEAD)
        head = step * heads + j
        whole_head = core * (steps * heads) + head
        bias = [bias_ref[n, whole_head] for n in range(3)]
        q, sq, c, sc = q_ref[:, cols], sq_ref[:, cols], c_ref[:, cols], sc_ref[:, cols]
        k_near = jnp.concatenate([k_ref[:, cols], sk_ref[:, cols]], axis=0)
        v_near = jnp.concatenate([v_ref[:, cols], sv_ref[:, cols]], axis=0)
        xk, xv, sxk, sxv = (
            ref[:, cols] for ref in (xk_ref, xv_ref, sxk_ref, sxv_ref)
        )
        k_one, v_one = split_rows(level_ref[:, 0:16, cols])
        k_two, v_two = split_rows(level_ref[:, 16:32, cols])
        k_far = jnp.concatenate([k_one, k_two], axis=0)
        v_far = jnp.concatenate([v_one, v_two], axis=0)
        q_both = jnp.concatenate([q, sq], axis=0)
        c_both = jnp.concatenate([c, sc], axis=0)

        s_near = nt(k_near, q_both) * scale + bias[0]
        s_edge = jnp.concatenate([nt(xk, q), nt(sxk, sq)], axis=1) * scale + (
            edge_ref[0:1] + bias[0]
        )
        s_far = nt(k_far, q_both) * scale
        s_one = s_far[0:ROWS] + (mask_ref[0:ROWS] + bias[1])
        s_two = s_far[ROWS:] + (mask_ref[ROWS:] + bias[2])
        scores = [s_near, s_edge, s_one, s_two]
        top = functools.reduce(
            jnp.maximum, [jnp.max(s, axis=0, keepdims=True) for s in scores]
        )
        powers = [jnp.exp(s - top) for s in scores]
        total = sum(jnp.sum(p, axis=0, keepdims=True) for p in powers)
        share = 1.0 / total
        weights = [p * share for p in powers]

        g_far = nt(v_far, c_both)
        grads = [
            nt(v_near, c_both),
            jnp.concatenate([nt(xv, c), nt(sxv, sc)], axis=1),
            g_far[0:ROWS],
            g_far[ROWS:],
        ]
        delta = sum(
            jnp.sum(w * g, axis=0, keepdims=True) for w, g in zip(weights, grads)
        )
        score_grads = [w * (g - delta) for w, g in zip(weights, grads)]
        w_near, w_edge, w_one, w_two = [w.astype(BF) for w in weights]
        d_near, d_edge, d_one, d_two = [d.astype(BF) for d in score_grads]
        w_far = jnp.concatenate([w_one, w_two], axis=0)
        d_far = jnp.concatenate([d_one, d_two], axis=0)

        att = tn(w_near, v_near) + tn(w_far, v_far)
        att_ref[:, cols] = (att[0:ROWS] + tn(w_edge[:, 0:ROWS], xv)).astype(BF)
        satt_ref[:, cols] = (att[ROWS:] + tn(w_edge[:, ROWS:], sxv)).astype(BF)
        dq = tn(d_near, k_near) + tn(d_far, k_far)
        dq_ref[:, cols] = ((dq[0:ROWS] + tn(d_edge[:, 0:ROWS], xk)) * scale).astype(BF)
        sdq_ref[:, cols] = ((dq[ROWS:] + tn(d_edge[:, ROWS:], sxk)) * scale).astype(BF)

        dk = nn(d_near, q_both) * scale
        dk_ref[:, cols] = dk[0:ROWS]
        sdk_ref[:, cols] = dk[ROWS:]
        dv = nn(w_near, c_both)
        dv_ref[:, cols] = dv[0:ROWS]
        sdv_ref[:, cols] = dv[ROWS:]
        dk = nn(d_far, q_both) * scale
        dv = nn(w_far, c_both)
        glevel_ref[:, 0:16, cols] = join_rows(dk[0:ROWS], dv[0:ROWS])
        sums = [jnp.sum(d, axis=0, keepdims=True) for d in score_grads]
        level = pieces([sums[0] + sums[1], sums[2], sums[3]])
        first = lax.broadcasted_iota(jnp.int32, (ROWS, HEAD), 0) % 8 == 0
        glevel_ref[:, 16:32, cols] = join_rows(
            jnp.where(first, level, dk[ROWS:]), dv[ROWS:]
        )

        log_total = top + jnp.log(total)
        row = pl.ds(head, 1)
        low = pl.ds(head + 8, 1)
        stat_ref[row] = log_total[:, 0:ROWS]
        sstat_ref[row] = log_total[:, ROWS:]
        stat_ref[low] = delta[:, 0:ROWS]
        sstat_ref[low] = delta[:, ROWS:]


def attend(ids, bias, own, sib, x, sx, level):
    width = own[0].shape[1]
    half = width // 2
    heads = 2
    block = heads * HEAD
    steps = half // block
    rows = ROWS

    def mine(n, at=0):
        return pl.BlockSpec((n, block), lambda i, ids: (at, ids[1] * steps + i))

    def part(n, at=0):
        return pl.BlockSpec((n, block), lambda i, ids: (at, i))

    rows_of = pl.BlockSpec((GROUP, 32, block), lambda i, ids: (0, 0, i))
    stat = pl.BlockSpec((16, rows), lambda i, ids: (0, 0))
    low = jax.ShapeDtypeStruct((rows, half), BF)
    high = jax.ShapeDtypeStruct((rows, half), F32)
    stats = jax.ShapeDtypeStruct((16, rows), F32)
    return pl.pallas_call(
        functools.partial(attend_kernel, steps, heads),
        grid_spec=pltpu.PrefetchScalarGridSpec(
            num_scalar_prefetch=1,
            grid=(steps,),
            in_specs=[pl.BlockSpec(memory_space=pltpu.SMEM)]
            + [mine(rows)] * 4
            + [part(rows)] * 4
            + [mine(rows), mine(rows, 1), part(rows), part(rows, 1)]
            + [rows_of],
            out_specs=[part(rows)] * 8 + [rows_of] + [stat] * 2,
            scratch_shapes=[
                pltpu.VMEM((2 * rows, 2 * rows), F32),
                pltpu.VMEM((8, 2 * rows), F32),
            ],
        ),
        out_shape=out_hbm(
            [low] * 4
            + [high] * 4
            + [jax.ShapeDtypeStruct((GROUP, 32, half), BF)]
            + [stats] * 2
        ),
        compiler_params=params(),
        cost_estimate=cost(9),
    )(ids, bias, *in_hbm(*own, *sib, x, x, sx, sx, level))


def edge_kernel(
    per_half,
    heads,
    ids_ref,
    bias_ref,
    k_ref,
    v_ref,
    q_ref,
    c_ref,
    stat_ref,
    att_ref,
    satt_ref,
    dq_ref,
    sdq_ref,
    dk_ref,
    sdk_ref,
    dv_ref,
    sdv_ref,
    out_att_ref,
    out_dq_ref,
    out_dk_ref,
    out_dv_ref,
):
    step = pl.program_id(0)
    mine = step // per_half == ids_ref[1]
    scale = HEAD**-0.5
    out_att_ref[...] = jnp.where(mine, att_ref[...], satt_ref[...])
    out_dq_ref[...] = jnp.where(mine, dq_ref[...], sdq_ref[...])
    for j in range(heads):
        cols = slice(j * HEAD, (j + 1) * HEAD)
        bias = bias_ref[0, step * heads + j]
        row = lax.rem(step, per_half) * heads + j
        log_total = stat_ref[0, pl.ds(row, 1)]
        delta = stat_ref[0, pl.ds(row + 8, 1)]
        q, c = q_ref[:, cols], c_ref[:, cols]
        weights = jnp.exp(nt(k_ref[:, cols], q) * scale + (bias - log_total))
        score_grad = weights * (nt(v_ref[:, cols], c) - delta)
        dk = jnp.where(mine, dk_ref[:, cols], sdk_ref[:, cols])
        dv = jnp.where(mine, dv_ref[:, cols], sdv_ref[:, cols])
        out_dk_ref[:, cols] = dk + nn(score_grad.astype(BF), q) * scale
        out_dv_ref[:, cols] = dv + nn(weights.astype(BF), c)


def edge(ids, bias, k, v, x, stat, parts):
    rows, width = k.shape
    heads = 4
    block = heads * HEAD
    per_half = width // 2 // block
    whole = pl.BlockSpec((rows, block), lambda i, ids: (0, i))
    part = pl.BlockSpec((rows, block), lambda i, ids: (0, lax.rem(i, per_half)))
    return pl.pallas_call(
        functools.partial(edge_kernel, per_half, heads),
        grid_spec=pltpu.PrefetchScalarGridSpec(
            num_scalar_prefetch=1,
            grid=(2 * per_half,),
            in_specs=[
                pl.BlockSpec(memory_space=pltpu.SMEM),
                whole,
                whole,
                pl.BlockSpec((rows, block), lambda i, ids: (0, i)),
                pl.BlockSpec((rows, block), lambda i, ids: (1, i)),
                pl.BlockSpec((1, 16, rows), lambda i, ids: (i // per_half, 0, 0)),
            ]
            + [part] * 8,
            out_specs=[whole] * 4,
        ),
        out_shape=out_hbm(
            [jax.ShapeDtypeStruct((rows, width), t) for t in (BF, BF, F32, F32)]
        ),
        compiler_params=params(),
        cost_estimate=cost(4),
    )(ids, bias, *in_hbm(k, v, x, x, stat, *parts))


def sums_kernel(x_ref, one_ref, low_ref, high_ref, level_ref):
    total = jnp.sum(x_ref[:, 0].astype(F32), axis=0)
    one_ref[...] = total[0:16]
    zero = jnp.zeros((1, total.shape[-1]), F32)
    for n in range(2):
        at = 16 + 8 * n
        for r in range(4):
            row = total[at + r : at + r + 1]
            low_ref[r, n : n + 1, :] = row if r else zero
            high_ref[r, n : n + 1, :] = total[at + 4 + r : at + 5 + r]
        row = total[at : at + 1]
        high_ref[4, n : n + 1, :] = row
        level_ref[0, n : n + 1, :] = row


def sums(x):
    half = x.shape[-1]
    block = 512
    per_half = half // block
    x = x.reshape(GROUP // 2, 2, 32, half)
    return pl.pallas_call(
        sums_kernel,
        grid=(2 * per_half,),
        in_specs=[
            pl.BlockSpec(
                (GROUP // 2, 1, 32, block),
                lambda i: (0, i // per_half, 0, lax.rem(i, per_half)),
            )
        ],
        out_specs=[pl.BlockSpec((16, block), lambda i: (0, i))]
        + [pl.BlockSpec((n, 2, block), lambda i: (0, 0, i)) for n in (4, 5, 1)],
        out_shape=[jax.ShapeDtypeStruct((16, 2 * half), F32)]
        + [jax.ShapeDtypeStruct((n, 2, 2 * half), F32) for n in (4, 5, 1)],
        compiler_params=params(),
        cost_estimate=cost(1),
    )(x)


def final_kernel(one_ref, far_ref, dk_ref, dv_ref, out_dk_ref, out_dv_ref):
    total = one_ref[...] / POOL1
    for n, (ref, out) in enumerate(((dk_ref, out_dk_ref), (dv_ref, out_dv_ref))):
        rows = total[8 * n : 8 * n + 8] + far_ref[0, n : n + 1, :] / POOL2
        for r in range(8):
            at = slice(r * POOL1, (r + 1) * POOL1)
            out[at] = (ref[at] + rows[r : r + 1]).astype(BF)


def final(one, far, dk, dv):
    rows, width = dk.shape
    block = 512
    whole = pl.BlockSpec((rows, block), lambda i: (0, i))
    return pl.pallas_call(
        final_kernel,
        grid=(width // block,),
        in_specs=[
            pl.BlockSpec((16, block), lambda i: (0, i)),
            pl.BlockSpec((1, 2, block), lambda i: (0, 0, i)),
            whole,
            whole,
        ],
        out_specs=[whole] * 2,
        out_shape=[jax.ShapeDtypeStruct((rows, width), BF)] * 2,
        compiler_params=params(),
        cost_estimate=cost(2),
    )(one, far, dk, dv)


def body(queries, key_rows, values, cotangent, level_bias):
    q, k, v, c = queries[0], key_rows[0], values[0], cotangent[0]
    heads = level_bias.shape[1]
    size = lax.axis_size("seq")
    me = lax.axis_index("seq")
    core = me % 2
    ids = jnp.stack([me, core, size]).astype(jnp.int32)

    one, far = pool(k, v)
    far = jnp.concatenate([far, swap(far, Z1)], axis=0)
    far = jnp.concatenate([far, swap(far, YA)], axis=0)
    rows = level_rows(one, far, swap(far, YB))

    kv, qc, *sends = prepare(ids, k, v, q, c)
    sk, sv, sq, sc = [swap(s, SIB) for s in sends]
    x = cross(kv)
    rows, x = lax.optimization_barrier((rows, x))
    rows = in_group(rows)
    sx = swap(other_half(ids, x, 2 * ROWS), SIB)
    late, rows = lax.optimization_barrier((qc, rows))
    x_qc = cross(late)

    att, satt, dq, sdq, dk, dv, sdk, sdv, grads, stat, sstat = attend(
        ids, level_bias, (q, k, v, c), (sq, sk, sv, sc), x, sx, rows
    )

    grads, x_qc = lax.optimization_barrier((grads, x_qc))
    one, low, high, level = sums(in_group(grads))
    for mask in (YB, YA, Z1):
        got = swap(high, mask)
        low = low + got[:-1]
        level = level + got[-1:]
        half = low.shape[0] // 2
        high = jnp.concatenate([low[half:], level], axis=0)
        low = low[:half] if half else low

    rstat = swap(sstat, SIB)
    stats = jnp.where(core == 0, jnp.stack([stat, rstat]), jnp.stack([rstat, stat]))
    x_stats = cross(stats)
    ratt, rdq, rdk, rdv = [swap(s, SIB) for s in (satt, sdq, sdk, sdv)]
    att, dq, dk, dv = edge(
        ids,
        level_bias,
        k,
        v,
        x_qc,
        x_stats,
        (att, ratt, dq, rdq, dk, rdk, dv, rdv),
    )

    level = level + lax.ppermute(level, "batch", [(0, 1), (1, 0)])
    dk, dv = final(one, low, dk, dv)
    level = level[0, 0].reshape(heads, HEAD)[:, :9].reshape(heads, 3, 3).sum(1).T
    return att[None], dq[None], dk[None], dv[None], level


def solution(mesh):
    rows = P("batch", "seq", None)
    return jax.shard_map(
        body,
        mesh=mesh,
        in_specs=(rows, rows, rows, rows, P()),
        out_specs=(rows, rows, rows, rows, P()),
        check_vma=False,
    )
```

```python
import functools
import math

import jax
import jax.numpy as jnp
from jax import lax
from jax.experimental import pallas as pl
from jax.experimental.pallas import tpu as pltpu
from jax.sharding import PartitionSpec as P

POOL1 = 16
POOL2 = 128
GROUP = 16
ROWS = 128
HEAD = 128
NEGATIVE = -1e30
LOG2E = math.log2(math.e)
LOG1 = math.log2(POOL1)
LOG2 = math.log2(POOL2)

SIB, Z1, YA, YB = 1, 16, 32, 96

BF = jnp.bfloat16
F32 = jnp.float32


def swap(x, mask):
    return lax.ppermute(x, "seq", [(i, i ^ mask) for i in range(lax.axis_size("seq"))])


def cross(x):
    size = lax.axis_size("seq")
    pairs = [(i, i + 1) for i in range(1, size - 1, 2)]
    return lax.ppermute(x, "seq", pairs + [(j, i) for i, j in pairs])


def in_group(x):
    size = lax.axis_size("seq")
    groups = [[g + i for i in range(GROUP)] for g in range(0, size, GROUP)]
    return lax.all_to_all(x, "seq", 0, 0, axis_index_groups=groups)


def params(limit=24):
    return pltpu.CompilerParams(vmem_limit_bytes=limit * 1024 * 1024)


def cost(us):
    return pl.CostEstimate(flops=0, bytes_accessed=int(us * 3.3e6), transcendentals=0)


def in_hbm(*arrays):
    return [pltpu.with_memory_space_constraint(x, pltpu.HBM) for x in arrays]


def out_hbm(shapes):
    return [pltpu.HBM(s.shape, s.dtype) for s in shapes]


def nt(a, b):
    return lax.dot_general(a, b, (((1,), (1,)), ((), ())), preferred_element_type=F32)


def nn(a, b):
    return lax.dot_general(a, b, (((1,), (0,)), ((), ())), preferred_element_type=F32)


def tn(a, b):
    return lax.dot_general(a, b, (((0,), (0,)), ((), ())), preferred_element_type=F32)


def pool_kernel(k_ref, v_ref, one_ref, two_ref):
    for n, ref in enumerate((k_ref, v_ref)):
        x = ref[...].astype(F32)
        sums = jnp.sum(x.reshape(ROWS // POOL1, POOL1, x.shape[-1]), axis=1)
        one_ref[8 * n : 8 * n + 8, :] = sums / POOL1
        row = jnp.sum(sums, axis=0, keepdims=True) / POOL2
        two_ref[0, n : n + 1, :] = row.astype(BF)


def pool(k, v):
    width = k.shape[1]
    return pl.pallas_call(
        pool_kernel,
        out_shape=(
            jax.ShapeDtypeStruct((16, width), F32),
            jax.ShapeDtypeStruct((1, 2, width), BF),
        ),
        compiler_params=params(),
        cost_estimate=cost(2),
    )(k, v)


def rows_kernel(one_ref, a_ref, b_ref, out_ref, far_ref):
    half = out_ref.shape[-1]
    for m, ref in enumerate((a_ref, b_ref)):
        for r in range(4):
            pair = ref[r].astype(F32)
            for n in range(2):
                to = 8 * n + 4 * m + r
                far_ref[to : to + 1, :] = pair[n : n + 1, :]
    for c in range(2):
        cols = slice(c * half, (c + 1) * half)
        one = one_ref[:, cols].astype(BF)
        far = far_ref[:, cols].astype(BF)
        for p in range(GROUP // 2):
            out_ref[2 * p + c, 0:16] = one
            out_ref[2 * p + c, 16:32] = far


def level_rows(one, a, b):
    width = one.shape[1]
    return pl.pallas_call(
        rows_kernel,
        out_shape=jax.ShapeDtypeStruct((GROUP, 32, width // 2), BF),
        scratch_shapes=[pltpu.VMEM((16, width), F32)],
        compiler_params=params(),
        cost_estimate=cost(1),
    )(one, a, b)


def prepare_kernel(ids_ref, *refs):
    arrays, wholes, halves, sems = refs[:4], refs[4:6], refs[6:10], refs[10]
    half = halves[0].shape[-1]
    start = pl.multiple_of((1 - ids_ref[1]) * half, half)
    copies = []
    for n, (ref, out) in enumerate(zip(arrays, halves)):
        part = ref.at[:, pl.ds(start, half)]
        copies.append(pltpu.make_async_copy(part, out, sems.at[n]))
    for n, ref in enumerate(arrays):
        to = wholes[n // 2].at[(n % 2) * ROWS : (n % 2 + 1) * ROWS]
        copies.append(pltpu.make_async_copy(ref, to, sems.at[4 + n]))
    for copy in copies:
        copy.start()
    for copy in copies:
        copy.wait()


def prepare(ids, *arrays):
    rows, width = arrays[0].shape
    smem = pl.BlockSpec(memory_space=pltpu.SMEM)
    hbm = pl.BlockSpec(memory_space=pltpu.HBM)
    return pl.pallas_call(
        prepare_kernel,
        in_specs=[smem] + [hbm] * 4,
        out_specs=[hbm] * 6,
        out_shape=[jax.ShapeDtypeStruct((2 * rows, width), BF)] * 2
        + [jax.ShapeDtypeStruct((rows, width // 2), BF)] * 4,
        scratch_shapes=[pltpu.SemaphoreType.DMA((8,))],
        compiler_params=params(),
        cost_estimate=cost(1),
    )(ids, *in_hbm(*arrays))


def other_kernel(ids_ref, x_ref, out_ref, sem):
    half = out_ref.shape[-1]
    start = pl.multiple_of((1 - ids_ref[1]) * half, half)
    copy = pltpu.make_async_copy(x_ref.at[:, pl.ds(start, half)], out_ref, sem)
    copy.start()
    copy.wait()


def other_half(ids, x):
    smem = pl.BlockSpec(memory_space=pltpu.SMEM)
    hbm = pl.BlockSpec(memory_space=pltpu.HBM)
    return pl.pallas_call(
        other_kernel,
        in_specs=[smem, hbm],
        out_specs=hbm,
        out_shape=jax.ShapeDtypeStruct((x.shape[0], x.shape[1] // 2), BF),
        scratch_shapes=[pltpu.SemaphoreType.DMA],
        compiler_params=params(),
        cost_estimate=cost(12),
    )(ids, x)


def split_rows(x):
    wide = x.astype(F32).reshape(GROUP, 16, HEAD)
    keys = wide[:, :8].reshape(ROWS, HEAD).astype(BF)
    return keys, wide[:, 8:].reshape(ROWS, HEAD).astype(BF)


def join_rows(a, b):
    both = [x.reshape(GROUP, 8, HEAD) for x in (a, b)]
    return jnp.concatenate(both, axis=1).astype(BF)


def pieces(sums):
    lane = lax.broadcasted_iota(jnp.int32, (1, HEAD), 1)
    row = jnp.zeros((1, HEAD), F32)
    for n, s in enumerate(sums):
        row = jnp.where(lane % 3 == n, jnp.sum(s, axis=1, keepdims=True), row)
    high = row.astype(BF).astype(F32)
    middle = (row - high).astype(BF).astype(F32)
    rest = row - high - middle
    row = jnp.where(lane < 3, high, jnp.where(lane < 6, middle, rest))
    return jnp.where(lane < 9, row, 0.0)


def attend_kernel(
    steps,
    heads,
    ids_ref,
    bias_ref,
    q_ref,
    k_ref,
    v_ref,
    c_ref,
    sq_ref,
    sk_ref,
    sv_ref,
    sc_ref,
    xk_ref,
    xv_ref,
    sxk_ref,
    sxv_ref,
    level_ref,
    att_ref,
    satt_ref,
    dq_ref,
    sdq_ref,
    dk_ref,
    dv_ref,
    sdk_ref,
    sdv_ref,
    glevel_ref,
    stat_ref,
    sstat_ref,
    mask_ref,
    edge_ref,
):
    step = pl.program_id(0)
    me, core = ids_ref[0], ids_ref[1]
    last = ids_ref[2] - 1
    scale = HEAD**-0.5
    unit = scale * LOG2E

    @pl.when(step == 0)
    def _():
        row = lax.broadcasted_iota(jnp.int32, (ROWS, 2 * ROWS), 0)
        lane = lax.broadcasted_iota(jnp.int32, (ROWS, 2 * ROWS), 1)
        block = jnp.where(lane < ROWS, me, me ^ 1)
        group = me // GROUP
        place, which = row // 8, row % 8
        good = jnp.abs(group * GROUP + place - block) >= 2
        mask_ref[0:ROWS] = jnp.where(good, LOG1, NEGATIVE)
        owner = (group ^ (which ^ ((which >> 2) << 1))) * GROUP + place
        good = (which != 0) & (jnp.abs(owner - block) >= 2)
        mask_ref[ROWS:] = jnp.where(good, LOG2, NEGATIVE)
        lane = lane[0:8]
        block = block[0:8]
        edge_ref[...] = jnp.where((block == 0) | (block == last), NEGATIVE, 0.0)

    for j in range(heads):
        cols = slice(j * HEAD, (j + 1) * HEAD)
        head = step * heads + j
        whole_head = core * (steps * heads) + head
        bias = [bias_ref[n, whole_head] * LOG2E for n in range(3)]
        q, sq, c, sc = q_ref[:, cols], sq_ref[:, cols], c_ref[:, cols], sc_ref[:, cols]
        k_near = jnp.concatenate([k_ref[:, cols], sk_ref[:, cols]], axis=0)
        v_near = jnp.concatenate([v_ref[:, cols], sv_ref[:, cols]], axis=0)
        xk, xv, sxk, sxv = (
            ref[:, cols] for ref in (xk_ref, xv_ref, sxk_ref, sxv_ref)
        )
        k_one, v_one = split_rows(level_ref[:, 0:16, cols])
        k_two, v_two = split_rows(level_ref[:, 16:32, cols])
        k_far = jnp.concatenate([k_one, k_two], axis=0)
        v_far = jnp.concatenate([v_one, v_two], axis=0)
        q_both = jnp.concatenate([q, sq], axis=0)
        c_both = jnp.concatenate([c, sc], axis=0)

        near = nt(k_near, q_both)
        edge = jnp.concatenate([nt(xk, q), nt(sxk, sq)], axis=1)
        far = nt(k_far, q_both) * unit + mask_ref[...]
        parts = [near, edge, far[0:ROWS], far[ROWS:]]
        shifts = [bias[0], bias[0] + edge_ref[0:1], bias[1], bias[2]]
        tops = [jnp.max(x, axis=0, keepdims=True) for x in parts]
        tops = [t * unit for t in tops[:2]] + tops[2:]
        top = functools.reduce(jnp.maximum, [t + s for t, s in zip(tops, shifts)])
        parts = [x * unit for x in parts[:2]] + parts[2:]
        powers = [jnp.exp2(x + (s - top)) for x, s in zip(parts, shifts)]
        masses = [jnp.sum(p, axis=0, keepdims=True) for p in powers]
        total = sum(masses)
        share = 1.0 / total
        weights = [p * share for p in powers]

        g_far = nt(v_far, c_both)
        grads = [
            nt(v_near, c_both),
            jnp.concatenate([nt(xv, c), nt(sxv, sc)], axis=1),
            g_far[0:ROWS],
            g_far[ROWS:],
        ]
        deltas = [
            jnp.sum(w * g, axis=0, keepdims=True) for w, g in zip(weights, grads)
        ]
        delta = sum(deltas)
        score_grads = [w * (g - delta) for w, g in zip(weights, grads)]
        w_near, w_edge, w_one, w_two = [w.astype(BF) for w in weights]
        d_near, d_edge, d_one, d_two = [d.astype(BF) for d in score_grads]
        w_far = jnp.concatenate([w_one, w_two], axis=0)
        d_far = jnp.concatenate([d_one, d_two], axis=0)

        att = tn(w_near, v_near) + tn(w_far, v_far)
        att_ref[:, cols] = (att[0:ROWS] + tn(w_edge[:, 0:ROWS], xv)).astype(BF)
        satt_ref[:, cols] = (att[ROWS:] + tn(w_edge[:, ROWS:], sxv)).astype(BF)
        dq = tn(d_near, k_near) + tn(d_far, k_far)
        dq_ref[:, cols] = ((dq[0:ROWS] + tn(d_edge[:, 0:ROWS], xk)) * scale).astype(BF)
        sdq_ref[:, cols] = ((dq[ROWS:] + tn(d_edge[:, ROWS:], sxk)) * scale).astype(BF)

        dk = nn(d_near, q_both) * scale
        dk_ref[:, cols] = dk[0:ROWS]
        sdk_ref[:, cols] = dk[ROWS:]
        dv = nn(w_near, c_both)
        dv_ref[:, cols] = dv[0:ROWS]
        sdv_ref[:, cols] = dv[ROWS:]
        dk = nn(d_far, q_both) * scale
        dv = nn(w_far, c_both)
        glevel_ref[:, 0:16, cols] = join_rows(dk[0:ROWS], dv[0:ROWS])
        loads = [d - m * (share * delta) for d, m in zip(deltas, masses)]
        level = pieces([loads[0] + loads[1], loads[2], loads[3]])
        first = lax.broadcasted_iota(jnp.int32, (ROWS, HEAD), 0) % 8 == 0
        glevel_ref[:, 16:32, cols] = join_rows(
            jnp.where(first, level, dk[ROWS:]), dv[ROWS:]
        )

        log_total = top + jnp.log(total) * LOG2E
        row = pl.ds(head, 1)
        low = pl.ds(head + 8, 1)
        stat_ref[row] = log_total[:, 0:ROWS]
        sstat_ref[row] = log_total[:, ROWS:]
        stat_ref[low] = delta[:, 0:ROWS]
        sstat_ref[low] = delta[:, ROWS:]


def attend(ids, bias, own, sib, x, sx, level):
    width = own[0].shape[1]
    half = width // 2
    heads = 2
    block = heads * HEAD
    steps = half // block
    rows = ROWS

    def mine(n, at=0):
        return pl.BlockSpec((n, block), lambda i, ids: (at, ids[1] * steps + i))

    def part(n, at=0):
        return pl.BlockSpec((n, block), lambda i, ids: (at, i))

    rows_of = pl.BlockSpec((GROUP, 32, block), lambda i, ids: (0, 0, i))
    stat = pl.BlockSpec((16, rows), lambda i, ids: (0, 0))
    low = jax.ShapeDtypeStruct((rows, half), BF)
    high = jax.ShapeDtypeStruct((rows, half), F32)
    stats = jax.ShapeDtypeStruct((16, rows), F32)
    return pl.pallas_call(
        functools.partial(attend_kernel, steps, heads),
        grid_spec=pltpu.PrefetchScalarGridSpec(
            num_scalar_prefetch=1,
            grid=(steps,),
            in_specs=[pl.BlockSpec(memory_space=pltpu.SMEM)]
            + [mine(rows)] * 4
            + [part(rows)] * 4
            + [mine(rows), mine(rows, 1), part(rows), part(rows, 1)]
            + [rows_of],
            out_specs=[part(rows)] * 8 + [rows_of] + [stat] * 2,
            scratch_shapes=[
                pltpu.VMEM((2 * rows, 2 * rows), F32),
                pltpu.VMEM((8, 2 * rows), F32),
            ],
        ),
        out_shape=out_hbm(
            [low] * 4
            + [high] * 4
            + [jax.ShapeDtypeStruct((GROUP, 32, half), BF)]
            + [stats] * 2
        ),
        compiler_params=params(),
        cost_estimate=cost(9),
    )(ids, bias, *in_hbm(*own, *sib, x, x, sx, sx), level)


def edge_kernel(
    per_half,
    heads,
    ids_ref,
    bias_ref,
    k_ref,
    v_ref,
    q_ref,
    c_ref,
    stat_ref,
    att_ref,
    satt_ref,
    dq_ref,
    sdq_ref,
    dk_ref,
    sdk_ref,
    dv_ref,
    sdv_ref,
    out_att_ref,
    out_dq_ref,
    out_dk_ref,
    out_dv_ref,
):
    step = pl.program_id(0)
    mine = step // per_half == ids_ref[1]
    scale = HEAD**-0.5
    out_att_ref[...] = jnp.where(mine, att_ref[...], satt_ref[...])
    out_dq_ref[...] = jnp.where(mine, dq_ref[...], sdq_ref[...])
    for j in range(heads):
        cols = slice(j * HEAD, (j + 1) * HEAD)
        bias = bias_ref[0, step * heads + j] * LOG2E
        row = lax.rem(step, per_half) * heads + j
        log_total = stat_ref[0, pl.ds(row, 1)]
        delta = stat_ref[0, pl.ds(row + 8, 1)]
        q, c = q_ref[:, cols], c_ref[:, cols]
        score = nt(k_ref[:, cols], q) * (scale * LOG2E)
        weights = jnp.exp2(score + (bias - log_total))
        score_grad = weights * (nt(v_ref[:, cols], c) - delta)
        dk = jnp.where(mine, dk_ref[:, cols], sdk_ref[:, cols])
        dv = jnp.where(mine, dv_ref[:, cols], sdv_ref[:, cols])
        out_dk_ref[:, cols] = dk + nn(score_grad.astype(BF), q) * scale
        out_dv_ref[:, cols] = dv + nn(weights.astype(BF), c)


def edge(ids, bias, k, v, x, stat, parts):
    rows, width = k.shape
    heads = 8
    block = heads * HEAD
    per_half = width // 2 // block
    whole = pl.BlockSpec((rows, block), lambda i, ids: (0, i))
    part = pl.BlockSpec((rows, block), lambda i, ids: (0, lax.rem(i, per_half)))
    return pl.pallas_call(
        functools.partial(edge_kernel, per_half, heads),
        grid_spec=pltpu.PrefetchScalarGridSpec(
            num_scalar_prefetch=1,
            grid=(2 * per_half,),
            in_specs=[
                pl.BlockSpec(memory_space=pltpu.SMEM),
                whole,
                whole,
                pl.BlockSpec((rows, block), lambda i, ids: (0, i)),
                pl.BlockSpec((rows, block), lambda i, ids: (1, i)),
                pl.BlockSpec((1, 16, rows), lambda i, ids: (i // per_half, 0, 0)),
            ]
            + [part] * 8,
            out_specs=[whole] * 4,
        ),
        out_shape=out_hbm([jax.ShapeDtypeStruct((rows, width), BF)] * 2)
        + [jax.ShapeDtypeStruct((rows, width), F32)] * 2,
        compiler_params=params(),
        cost_estimate=cost(14),
    )(ids, bias, *in_hbm(k, v, x, x, stat, *parts))


def sums_kernel(x_ref, one_ref, low_ref, high_ref, level_ref):
    total = jnp.sum(x_ref[:, 0].astype(F32), axis=0)
    one_ref[...] = total[0:16]
    zero = jnp.zeros((1, total.shape[-1]), F32)
    for n in range(2):
        at = 16 + 8 * n
        for r in range(4):
            row = total[at + r : at + r + 1]
            low_ref[r, n : n + 1, :] = row if r else zero
            high_ref[r, n : n + 1, :] = total[at + 4 + r : at + 5 + r]
        row = total[at : at + 1]
        high_ref[4, n : n + 1, :] = row
        level_ref[0, n : n + 1, :] = row


def sums(x):
    half = x.shape[-1]
    block = 512
    per_half = half // block
    x = x.reshape(GROUP // 2, 2, 32, half)
    return pl.pallas_call(
        sums_kernel,
        grid=(2 * per_half,),
        in_specs=[
            pl.BlockSpec(
                (GROUP // 2, 1, 32, block),
                lambda i: (0, i // per_half, 0, lax.rem(i, per_half)),
            )
        ],
        out_specs=[pl.BlockSpec((16, block), lambda i: (0, i))]
        + [pl.BlockSpec((n, 2, block), lambda i: (0, 0, i)) for n in (4, 5, 1)],
        out_shape=[jax.ShapeDtypeStruct((16, 2 * half), F32)]
        + [jax.ShapeDtypeStruct((n, 2, 2 * half), F32) for n in (4, 5, 1)],
        compiler_params=params(),
        cost_estimate=cost(1),
    )(x)


def step_kernel(low_ref, got_ref, level_ref, out_low_ref, out_high_ref, out_level_ref):
    count = low_ref.shape[0]
    half = count // 2
    out_low_ref[...] = low_ref[0:half] + got_ref[0:half]
    out_high_ref[0:half] = low_ref[half:count] + got_ref[half:count]
    level = level_ref[...] + got_ref[count:]
    out_level_ref[...] = level
    out_high_ref[half:] = level


def step(low, got, level):
    half, width = low.shape[0] // 2, low.shape[2]
    counts = (half, half + 1, 1)
    return pl.pallas_call(
        step_kernel,
        out_shape=[jax.ShapeDtypeStruct((n, 2, width), F32) for n in counts],
        compiler_params=params(),
        cost_estimate=cost(1),
    )(low, got, level)


def final_kernel(one_ref, far_ref, got_ref, dk_ref, dv_ref, out_dk_ref, out_dv_ref):
    total = one_ref[...] / POOL1
    for n, (ref, out) in enumerate(((dk_ref, out_dk_ref), (dv_ref, out_dv_ref))):
        far = far_ref[0, n : n + 1, :] + got_ref[0, n : n + 1, :]
        rows = total[8 * n : 8 * n + 8] + far / POOL2
        for r in range(8):
            at = slice(r * POOL1, (r + 1) * POOL1)
            out[at] = (ref[at] + rows[r : r + 1]).astype(BF)


def final(one, far, got, dk, dv):
    rows, width = dk.shape
    block = 512
    whole = pl.BlockSpec((rows, block), lambda i: (0, i))
    return pl.pallas_call(
        final_kernel,
        grid=(width // block,),
        in_specs=[
            pl.BlockSpec((16, block), lambda i: (0, i)),
            pl.BlockSpec((1, 2, block), lambda i: (0, 0, i)),
            pl.BlockSpec((2, 2, block), lambda i: (0, 0, i)),
            whole,
            whole,
        ],
        out_specs=[whole] * 2,
        out_shape=[jax.ShapeDtypeStruct((rows, width), BF)] * 2,
        compiler_params=params(),
        cost_estimate=cost(2),
    )(one, far, got, dk, dv)


def body(queries, key_rows, values, cotangent, level_bias):
    q, k, v, c = queries[0], key_rows[0], values[0], cotangent[0]
    heads = level_bias.shape[1]
    size = lax.axis_size("seq")
    me = lax.axis_index("seq")
    core = me % 2
    ids = jnp.stack([me, core, size]).astype(jnp.int32)

    kv, qc, *sends = prepare(ids, k, v, q, c)
    x = cross(kv)
    one, far = pool(k, v)
    far = jnp.concatenate([far, swap(far, Z1)], axis=0)
    far = jnp.concatenate([far, swap(far, YA)], axis=0)
    rows = level_rows(one, far, swap(far, YB))

    sk, sv, sq, sc = [swap(s, SIB) for s in sends]
    rows, x, sk, sv, sq, sc = lax.optimization_barrier((rows, x, sk, sv, sq, sc))
    rows = in_group(rows)
    sx = swap(other_half(ids, x), SIB)
    late, rows, sx = lax.optimization_barrier((qc, rows, sx))
    x_qc = cross(late)

    att, satt, dq, sdq, dk, dv, sdk, sdv, grads, stat, sstat = attend(
        ids, level_bias, (q, k, v, c), (sq, sk, sv, sc), x, sx, rows
    )

    grads, x_qc = lax.optimization_barrier((grads, x_qc))
    grads = in_group(grads)

    rstat = swap(sstat, SIB)
    stats = jnp.where(core == 0, jnp.stack([stat, rstat]), jnp.stack([rstat, stat]))
    x_stats = cross(stats)
    grads, x_stats = lax.optimization_barrier((grads, x_stats))
    ratt, rdq, rdk, rdv = [swap(s, SIB) for s in (satt, sdq, sdk, sdv)]
    att, dq, dk, dv = edge(
        ids,
        level_bias,
        k,
        v,
        x_qc,
        x_stats,
        (att, ratt, dq, rdq, dk, rdk, dv, rdv),
    )

    one, low, high, level = sums(grads)
    low, high, level = step(low, swap(high, YB), level)
    low, high, level = step(low, swap(high, YA), level)
    high, dk, dv = lax.optimization_barrier((high, dk, dv))
    got = swap(high, Z1)
    dk, dv = final(one, low, got, dk, dv)
    level = level + got[1:]
    level = level + lax.ppermute(level, "batch", [(0, 1), (1, 0)])
    level = level[0, 0].reshape(heads, HEAD)[:, :9].reshape(heads, 3, 3).sum(1).T
    return att[None], dq[None], dk[None], dv[None], level


def solution(mesh):
    rows = P("batch", "seq", None)
    return jax.shard_map(
        body,
        mesh=mesh,
        in_specs=(rows, rows, rows, rows, P()),
        out_specs=(rows, rows, rows, rows, P()),
        check_vma=False,
    )
```

```python
import functools
import math

import jax
import jax.numpy as jnp
from jax import lax
from jax.experimental import pallas as pl
from jax.experimental.pallas import tpu as pltpu
from jax.sharding import PartitionSpec as P

POOL1 = 16
POOL2 = 128
GROUP = 16
ROWS = 128
HEAD = 128
NEGATIVE = -1e30
LOG2E = math.log2(math.e)
LOG1 = math.log2(POOL1)
LOG2 = math.log2(POOL2)

SIB, Z1, YA, YB = 1, 16, 32, 96

BF = jnp.bfloat16
F32 = jnp.float32


def swap(x, mask):
    return lax.ppermute(x, "seq", [(i, i ^ mask) for i in range(lax.axis_size("seq"))])


def cross(x):
    size = lax.axis_size("seq")
    pairs = [(i, i + 1) for i in range(1, size - 1, 2)]
    return lax.ppermute(x, "seq", pairs + [(j, i) for i, j in pairs])


def in_group(x):
    size = lax.axis_size("seq")
    groups = [[g + i for i in range(GROUP)] for g in range(0, size, GROUP)]
    return lax.all_to_all(x, "seq", 0, 0, axis_index_groups=groups)


def params(limit=24):
    return pltpu.CompilerParams(vmem_limit_bytes=limit * 1024 * 1024)


def cost(us):
    return pl.CostEstimate(flops=0, bytes_accessed=int(us * 3.3e6), transcendentals=0)


def in_hbm(*arrays):
    return [pltpu.with_memory_space_constraint(x, pltpu.HBM) for x in arrays]


def out_hbm(shapes):
    return [pltpu.HBM(s.shape, s.dtype) for s in shapes]


def nt(a, b):
    return lax.dot_general(a, b, (((1,), (1,)), ((), ())), preferred_element_type=F32)


def nn(a, b):
    return lax.dot_general(a, b, (((1,), (0,)), ((), ())), preferred_element_type=F32)


def tn(a, b):
    return lax.dot_general(a, b, (((0,), (0,)), ((), ())), preferred_element_type=F32)


def pool_kernel(k_ref, v_ref, one_ref, two_ref):
    for n, ref in enumerate((k_ref, v_ref)):
        x = ref[...].astype(F32)
        sums = jnp.sum(x.reshape(ROWS // POOL1, POOL1, x.shape[-1]), axis=1)
        one_ref[8 * n : 8 * n + 8, :] = sums / POOL1
        row = jnp.sum(sums, axis=0, keepdims=True) / POOL2
        two_ref[0, n : n + 1, :] = row.astype(BF)


def pool(k, v):
    width = k.shape[1]
    return pl.pallas_call(
        pool_kernel,
        out_shape=(
            jax.ShapeDtypeStruct((16, width), F32),
            jax.ShapeDtypeStruct((1, 2, width), BF),
        ),
        compiler_params=params(),
        cost_estimate=cost(2),
    )(k, v)


def rows_kernel(one_ref, a_ref, b_ref, out_ref, far_ref):
    half = out_ref.shape[-1]
    for m, ref in enumerate((a_ref, b_ref)):
        for r in range(4):
            pair = ref[r].astype(F32)
            for n in range(2):
                to = 8 * n + 4 * m + r
                far_ref[to : to + 1, :] = pair[n : n + 1, :]
    for c in range(2):
        cols = slice(c * half, (c + 1) * half)
        one = one_ref[:, cols].astype(BF)
        far = far_ref[:, cols].astype(BF)
        for p in range(GROUP // 2):
            out_ref[2 * p + c, 0:16] = one
            out_ref[2 * p + c, 16:32] = far


def level_rows(one, a, b):
    width = one.shape[1]
    return pl.pallas_call(
        rows_kernel,
        out_shape=jax.ShapeDtypeStruct((GROUP, 32, width // 2), BF),
        scratch_shapes=[pltpu.VMEM((16, width), F32)],
        compiler_params=params(),
        cost_estimate=cost(1),
    )(one, a, b)


def prepare_kernel(ids_ref, *refs):
    arrays, wholes, halves, sems = refs[:4], refs[4:6], refs[6:10], refs[10]
    half = halves[0].shape[-1]
    start = pl.multiple_of((1 - ids_ref[1]) * half, half)
    copies = []
    for n, (ref, out) in enumerate(zip(arrays, halves)):
        part = ref.at[:, pl.ds(start, half)]
        copies.append(pltpu.make_async_copy(part, out, sems.at[n]))
    for n, ref in enumerate(arrays):
        to = wholes[n // 2].at[(n % 2) * ROWS : (n % 2 + 1) * ROWS]
        copies.append(pltpu.make_async_copy(ref, to, sems.at[4 + n]))
    for copy in copies:
        copy.start()
    for copy in copies:
        copy.wait()


def prepare(ids, *arrays):
    rows, width = arrays[0].shape
    smem = pl.BlockSpec(memory_space=pltpu.SMEM)
    hbm = pl.BlockSpec(memory_space=pltpu.HBM)
    return pl.pallas_call(
        prepare_kernel,
        in_specs=[smem] + [hbm] * 4,
        out_specs=[hbm] * 6,
        out_shape=[jax.ShapeDtypeStruct((2 * rows, width), BF)] * 2
        + [jax.ShapeDtypeStruct((rows, width // 2), BF)] * 4,
        scratch_shapes=[pltpu.SemaphoreType.DMA((8,))],
        compiler_params=params(),
        cost_estimate=cost(1),
    )(ids, *in_hbm(*arrays))


def other_kernel(ids_ref, x_ref, out_ref, sem):
    half = out_ref.shape[-1]
    start = pl.multiple_of((1 - ids_ref[1]) * half, half)
    copy = pltpu.make_async_copy(x_ref.at[:, pl.ds(start, half)], out_ref, sem)
    copy.start()
    copy.wait()


def other_half(ids, x):
    smem = pl.BlockSpec(memory_space=pltpu.SMEM)
    hbm = pl.BlockSpec(memory_space=pltpu.HBM)
    return pl.pallas_call(
        other_kernel,
        in_specs=[smem, hbm],
        out_specs=hbm,
        out_shape=jax.ShapeDtypeStruct((x.shape[0], x.shape[1] // 2), BF),
        scratch_shapes=[pltpu.SemaphoreType.DMA],
        compiler_params=params(),
        cost_estimate=cost(12),
    )(ids, x)


def split_rows(x):
    wide = x.astype(F32).reshape(GROUP, 16, HEAD)
    keys = wide[:, :8].reshape(ROWS, HEAD).astype(BF)
    return keys, wide[:, 8:].reshape(ROWS, HEAD).astype(BF)


def join_rows(a, b):
    both = [x.reshape(GROUP, 8, HEAD) for x in (a, b)]
    return jnp.concatenate(both, axis=1).astype(BF)


def pieces(sums):
    lane = lax.broadcasted_iota(jnp.int32, (1, HEAD), 1)
    row = jnp.zeros((1, HEAD), F32)
    for n, s in enumerate(sums):
        row = jnp.where(lane % 3 == n, jnp.sum(s, axis=1, keepdims=True), row)
    high = row.astype(BF).astype(F32)
    middle = (row - high).astype(BF).astype(F32)
    rest = row - high - middle
    row = jnp.where(lane < 3, high, jnp.where(lane < 6, middle, rest))
    return jnp.where(lane < 9, row, 0.0)


def attend_kernel(
    steps,
    heads,
    ids_ref,
    bias_ref,
    q_ref,
    k_ref,
    v_ref,
    c_ref,
    sq_ref,
    sk_ref,
    sv_ref,
    sc_ref,
    xk_ref,
    xv_ref,
    sxk_ref,
    sxv_ref,
    level_ref,
    att_ref,
    satt_ref,
    dq_ref,
    sdq_ref,
    dk_ref,
    dv_ref,
    sdk_ref,
    sdv_ref,
    glevel_ref,
    stat_ref,
    sstat_ref,
    mask_ref,
    edge_ref,
):
    step = pl.program_id(0)
    me, core = ids_ref[0], ids_ref[1]
    last = ids_ref[2] - 1
    scale = HEAD**-0.5
    unit = scale * LOG2E

    @pl.when(step == 0)
    def _():
        row = lax.broadcasted_iota(jnp.int32, (ROWS, 2 * ROWS), 0)
        lane = lax.broadcasted_iota(jnp.int32, (ROWS, 2 * ROWS), 1)
        block = jnp.where(lane < ROWS, me, me ^ 1)
        group = me // GROUP
        place, which = row // 8, row % 8
        good = jnp.abs(group * GROUP + place - block) >= 2
        mask_ref[0:ROWS] = jnp.where(good, LOG1, NEGATIVE)
        owner = (group ^ (which ^ ((which >> 2) << 1))) * GROUP + place
        good = (which != 0) & (jnp.abs(owner - block) >= 2)
        mask_ref[ROWS:] = jnp.where(good, LOG2, NEGATIVE)
        lane = lane[0:8]
        block = block[0:8]
        edge_ref[...] = jnp.where((block == 0) | (block == last), NEGATIVE, 0.0)

    def one_head(j):
        cols = slice(j * HEAD, (j + 1) * HEAD)
        head = step * heads + j
        whole_head = core * (steps * heads) + head
        bias = [bias_ref[n, whole_head] * LOG2E for n in range(3)]
        q, sq, c, sc = q_ref[:, cols], sq_ref[:, cols], c_ref[:, cols], sc_ref[:, cols]
        k_near = jnp.concatenate([k_ref[:, cols], sk_ref[:, cols]], axis=0)
        v_near = jnp.concatenate([v_ref[:, cols], sv_ref[:, cols]], axis=0)
        xk, xv, sxk, sxv = (
            ref[:, cols] for ref in (xk_ref, xv_ref, sxk_ref, sxv_ref)
        )
        k_one, v_one = split_rows(level_ref[:, 0:16, cols])
        k_two, v_two = split_rows(level_ref[:, 16:32, cols])
        k_far = jnp.concatenate([k_one, k_two], axis=0)
        v_far = jnp.concatenate([v_one, v_two], axis=0)
        q_both = jnp.concatenate([q, sq], axis=0)
        c_both = jnp.concatenate([c, sc], axis=0)

        near = nt(k_near, q_both)
        edge = jnp.concatenate([nt(xk, q), nt(sxk, sq)], axis=1)
        far = nt(k_far, q_both) * unit + mask_ref[...]
        yield
        parts = [near, edge, far[0:ROWS], far[ROWS:]]
        shifts = [bias[0], bias[0] + edge_ref[0:1], bias[1], bias[2]]
        tops = [jnp.max(x, axis=0, keepdims=True) for x in parts]
        tops = [t * unit for t in tops[:2]] + tops[2:]
        top = functools.reduce(jnp.maximum, [t + s for t, s in zip(tops, shifts)])
        parts = [x * unit for x in parts[:2]] + parts[2:]
        powers = [jnp.exp2(x + (s - top)) for x, s in zip(parts, shifts)]
        masses = [jnp.sum(p, axis=0, keepdims=True) for p in powers]
        total = sum(masses)
        share = 1.0 / total
        weights = [p * share for p in powers]

        yield
        g_far = nt(v_far, c_both)
        grads = [
            nt(v_near, c_both),
            jnp.concatenate([nt(xv, c), nt(sxv, sc)], axis=1),
            g_far[0:ROWS],
            g_far[ROWS:],
        ]
        yield
        deltas = [
            jnp.sum(w * g, axis=0, keepdims=True) for w, g in zip(weights, grads)
        ]
        delta = sum(deltas)
        score_grads = [w * (g - delta) for w, g in zip(weights, grads)]
        w_near, w_edge, w_one, w_two = [w.astype(BF) for w in weights]
        d_near, d_edge, d_one, d_two = [d.astype(BF) for d in score_grads]
        yield
        w_far = jnp.concatenate([w_one, w_two], axis=0)
        d_far = jnp.concatenate([d_one, d_two], axis=0)

        att = tn(w_near, v_near) + tn(w_far, v_far)
        att_ref[:, cols] = (att[0:ROWS] + tn(w_edge[:, 0:ROWS], xv)).astype(BF)
        satt_ref[:, cols] = (att[ROWS:] + tn(w_edge[:, ROWS:], sxv)).astype(BF)
        dq = tn(d_near, k_near) + tn(d_far, k_far)
        dq_ref[:, cols] = ((dq[0:ROWS] + tn(d_edge[:, 0:ROWS], xk)) * scale).astype(BF)
        sdq_ref[:, cols] = ((dq[ROWS:] + tn(d_edge[:, ROWS:], sxk)) * scale).astype(BF)

        yield
        dk = nn(d_near, q_both) * scale
        dk_ref[:, cols] = dk[0:ROWS]
        sdk_ref[:, cols] = dk[ROWS:]
        dv = nn(w_near, c_both)
        dv_ref[:, cols] = dv[0:ROWS]
        sdv_ref[:, cols] = dv[ROWS:]
        dk = nn(d_far, q_both) * scale
        dv = nn(w_far, c_both)
        glevel_ref[:, 0:16, cols] = join_rows(dk[0:ROWS], dv[0:ROWS])
        loads = [d - m * (share * delta) for d, m in zip(deltas, masses)]
        level = pieces([loads[0] + loads[1], loads[2], loads[3]])
        first = lax.broadcasted_iota(jnp.int32, (ROWS, HEAD), 0) % 8 == 0
        glevel_ref[:, 16:32, cols] = join_rows(
            jnp.where(first, level, dk[ROWS:]), dv[ROWS:]
        )

        log_total = top + jnp.log(total) * LOG2E
        row = pl.ds(head, 1)
        low = pl.ds(head + 8, 1)
        stat_ref[row] = log_total[:, 0:ROWS]
        sstat_ref[row] = log_total[:, ROWS:]
        stat_ref[low] = delta[:, 0:ROWS]
        sstat_ref[low] = delta[:, ROWS:]

    running = [one_head(j) for j in range(heads)]
    for turn in range(heads + 5):
        for j in range(heads):
            if 0 <= turn - j <= 5:
                next(running[j], None)


def attend(ids, bias, own, sib, x, sx, level):
    width = own[0].shape[1]
    half = width // 2
    heads = 4
    block = heads * HEAD
    steps = half // block
    rows = ROWS

    def mine(n, at=0):
        return pl.BlockSpec((n, block), lambda i, ids: (at, ids[1] * steps + i))

    def part(n, at=0):
        return pl.BlockSpec((n, block), lambda i, ids: (at, i))

    rows_of = pl.BlockSpec((GROUP, 32, block), lambda i, ids: (0, 0, i))
    stat = pl.BlockSpec((16, rows), lambda i, ids: (0, 0))
    low = jax.ShapeDtypeStruct((rows, half), BF)
    high = jax.ShapeDtypeStruct((rows, half), F32)
    stats = jax.ShapeDtypeStruct((16, rows), F32)
    return pl.pallas_call(
        functools.partial(attend_kernel, steps, heads),
        grid_spec=pltpu.PrefetchScalarGridSpec(
            num_scalar_prefetch=1,
            grid=(steps,),
            in_specs=[pl.BlockSpec(memory_space=pltpu.SMEM)]
            + [mine(rows)] * 4
            + [part(rows)] * 4
            + [mine(rows), mine(rows, 1), part(rows), part(rows, 1)]
            + [rows_of],
            out_specs=[part(rows)] * 8 + [rows_of] + [stat] * 2,
            scratch_shapes=[
                pltpu.VMEM((2 * rows, 2 * rows), F32),
                pltpu.VMEM((8, 2 * rows), F32),
            ],
        ),
        out_shape=out_hbm(
            [low] * 4
            + [high] * 4
            + [jax.ShapeDtypeStruct((GROUP, 32, half), BF)]
            + [stats] * 2
        ),
        compiler_params=params(),
        cost_estimate=cost(9),
    )(ids, bias, *in_hbm(*own, *sib, x, x, sx, sx), level)


def edge_kernel(
    per_half,
    heads,
    ids_ref,
    bias_ref,
    k_ref,
    v_ref,
    q_ref,
    c_ref,
    stat_ref,
    dk_ref,
    sdk_ref,
    dv_ref,
    sdv_ref,
    out_dk_ref,
    out_dv_ref,
):
    step = pl.program_id(0)
    mine = step // per_half == ids_ref[1]
    scale = HEAD**-0.5
    for j in range(heads):
        cols = slice(j * HEAD, (j + 1) * HEAD)
        bias = bias_ref[0, step * heads + j] * LOG2E
        row = lax.rem(step, per_half) * heads + j
        log_total = stat_ref[0, pl.ds(row, 1)]
        delta = stat_ref[0, pl.ds(row + 8, 1)]
        q, c = q_ref[:, cols], c_ref[:, cols]
        score = nt(k_ref[:, cols], q) * (scale * LOG2E)
        weights = jnp.exp2(score + (bias - log_total))
        score_grad = weights * (nt(v_ref[:, cols], c) - delta)
        dk = jnp.where(mine, dk_ref[:, cols], sdk_ref[:, cols])
        dv = jnp.where(mine, dv_ref[:, cols], sdv_ref[:, cols])
        out_dk_ref[:, cols] = dk + nn(score_grad.astype(BF), q) * scale
        out_dv_ref[:, cols] = dv + nn(weights.astype(BF), c)


def edge(ids, bias, k, v, x, stat, parts):
    rows, width = k.shape
    heads = 8
    block = heads * HEAD
    per_half = width // 2 // block
    whole = pl.BlockSpec((rows, block), lambda i, ids: (0, i))
    part = pl.BlockSpec((rows, block), lambda i, ids: (0, lax.rem(i, per_half)))
    return pl.pallas_call(
        functools.partial(edge_kernel, per_half, heads),
        grid_spec=pltpu.PrefetchScalarGridSpec(
            num_scalar_prefetch=1,
            grid=(2 * per_half,),
            in_specs=[
                pl.BlockSpec(memory_space=pltpu.SMEM),
                whole,
                whole,
                pl.BlockSpec((rows, block), lambda i, ids: (0, i)),
                pl.BlockSpec((rows, block), lambda i, ids: (1, i)),
                pl.BlockSpec((1, 16, rows), lambda i, ids: (i // per_half, 0, 0)),
            ]
            + [part] * 4,
            out_specs=[whole] * 2,
        ),
        out_shape=[jax.ShapeDtypeStruct((rows, width), F32)] * 2,
        compiler_params=params(),
        cost_estimate=cost(14),
    )(ids, bias, *in_hbm(k, v), x, x, *in_hbm(stat, *parts))


def join_kernel(ids_ref, att_ref, satt_ref, dq_ref, sdq_ref, out_att_ref, out_dq_ref):
    mine = pl.program_id(0) == ids_ref[1]
    out_att_ref[...] = jnp.where(mine, att_ref[...], satt_ref[...])
    out_dq_ref[...] = jnp.where(mine, dq_ref[...], sdq_ref[...])


def join(ids, *parts):
    rows, half = parts[0].shape
    part = pl.BlockSpec((rows, half), lambda i, ids: (0, 0))
    return pl.pallas_call(
        join_kernel,
        grid_spec=pltpu.PrefetchScalarGridSpec(
            num_scalar_prefetch=1,
            grid=(2,),
            in_specs=[part] * 4,
            out_specs=[pl.BlockSpec((rows, half), lambda i, ids: (0, i))] * 2,
        ),
        out_shape=out_hbm([jax.ShapeDtypeStruct((rows, 2 * half), BF)] * 2),
        compiler_params=params(),
        cost_estimate=cost(6),
    )(ids, *in_hbm(*parts))


def sums_kernel(x_ref, one_ref, low_ref, high_ref, level_ref):
    total = jnp.sum(x_ref[:, 0].astype(F32), axis=0)
    one_ref[...] = total[0:16]
    zero = jnp.zeros((1, total.shape[-1]), F32)
    for n in range(2):
        at = 16 + 8 * n
        for r in range(4):
            row = total[at + r : at + r + 1]
            low_ref[r, n : n + 1, :] = row if r else zero
            high_ref[r, n : n + 1, :] = total[at + 4 + r : at + 5 + r]
        row = total[at : at + 1]
        high_ref[4, n : n + 1, :] = row
        level_ref[0, n : n + 1, :] = row


def sums(x):
    half = x.shape[-1]
    block = 512
    per_half = half // block
    x = x.reshape(GROUP // 2, 2, 32, half)
    return pl.pallas_call(
        sums_kernel,
        grid=(2 * per_half,),
        in_specs=[
            pl.BlockSpec(
                (GROUP // 2, 1, 32, block),
                lambda i: (0, i // per_half, 0, lax.rem(i, per_half)),
            )
        ],
        out_specs=[pl.BlockSpec((16, block), lambda i: (0, i))]
        + [pl.BlockSpec((n, 2, block), lambda i: (0, 0, i)) for n in (4, 5, 1)],
        out_shape=[jax.ShapeDtypeStruct((16, 2 * half), F32)]
        + [jax.ShapeDtypeStruct((n, 2, 2 * half), F32) for n in (4, 5, 1)],
        compiler_params=params(),
        cost_estimate=cost(1),
    )(x)


def step_kernel(low_ref, got_ref, level_ref, out_low_ref, out_high_ref, out_level_ref):
    count = low_ref.shape[0]
    half = count // 2
    out_low_ref[...] = low_ref[0:half] + got_ref[0:half]
    out_high_ref[0:half] = low_ref[half:count] + got_ref[half:count]
    level = level_ref[...] + got_ref[count:]
    out_level_ref[...] = level
    out_high_ref[half:] = level


def step(low, got, level):
    half, width = low.shape[0] // 2, low.shape[2]
    counts = (half, half + 1, 1)
    return pl.pallas_call(
        step_kernel,
        out_shape=[jax.ShapeDtypeStruct((n, 2, width), F32) for n in counts],
        compiler_params=params(),
        cost_estimate=cost(1),
    )(low, got, level)


def final_kernel(one_ref, far_ref, got_ref, dk_ref, dv_ref, out_dk_ref, out_dv_ref):
    total = one_ref[...] / POOL1
    for n, (ref, out) in enumerate(((dk_ref, out_dk_ref), (dv_ref, out_dv_ref))):
        far = far_ref[0, n : n + 1, :] + got_ref[0, n : n + 1, :]
        rows = total[8 * n : 8 * n + 8] + far / POOL2
        for r in range(8):
            at = slice(r * POOL1, (r + 1) * POOL1)
            out[at] = (ref[at] + rows[r : r + 1]).astype(BF)


def final(one, far, got, dk, dv):
    rows, width = dk.shape
    block = 512
    whole = pl.BlockSpec((rows, block), lambda i: (0, i))
    return pl.pallas_call(
        final_kernel,
        grid=(width // block,),
        in_specs=[
            pl.BlockSpec((16, block), lambda i: (0, i)),
            pl.BlockSpec((1, 2, block), lambda i: (0, 0, i)),
            pl.BlockSpec((2, 2, block), lambda i: (0, 0, i)),
            whole,
            whole,
        ],
        out_specs=[whole] * 2,
        out_shape=[jax.ShapeDtypeStruct((rows, width), BF)] * 2,
        compiler_params=params(),
        cost_estimate=cost(2),
    )(one, far, got, dk, dv)


def body(queries, key_rows, values, cotangent, level_bias):
    q, k, v, c = queries[0], key_rows[0], values[0], cotangent[0]
    heads = level_bias.shape[1]
    size = lax.axis_size("seq")
    me = lax.axis_index("seq")
    core = me % 2
    ids = jnp.stack([me, core, size]).astype(jnp.int32)

    kv, qc, *sends = prepare(ids, k, v, q, c)
    x = cross(kv)
    one, far = pool(k, v)
    far = jnp.concatenate([far, swap(far, Z1)], axis=0)
    far = jnp.concatenate([far, swap(far, YA)], axis=0)
    rows = level_rows(one, far, swap(far, YB))

    sk, sv, sq, sc = [swap(s, SIB) for s in sends]
    rows, x, sk, sv, sq, sc = lax.optimization_barrier((rows, x, sk, sv, sq, sc))
    rows = in_group(rows)
    sx = swap(other_half(ids, x), SIB)
    late, rows, sx = lax.optimization_barrier((qc, rows, sx))
    x_qc = cross(late)

    att, satt, dq, sdq, dk, dv, sdk, sdv, grads, stat, sstat = attend(
        ids, level_bias, (q, k, v, c), (sq, sk, sv, sc), x, sx, rows
    )

    grads, x_qc = lax.optimization_barrier((grads, x_qc))
    grads = in_group(grads)

    rstat = swap(sstat, SIB)
    stats = jnp.where(core == 0, jnp.stack([stat, rstat]), jnp.stack([rstat, stat]))
    x_stats = cross(stats)
    grads, x_stats = lax.optimization_barrier((grads, x_stats))
    ratt, rdq, rdk, rdv = [swap(s, SIB) for s in (satt, sdq, sdk, sdv)]
    att, dq = join(ids, att, ratt, dq, rdq)
    grads, att, dq = lax.optimization_barrier((grads, att, dq))
    dk, dv = edge(ids, level_bias, k, v, x_qc, x_stats, (dk, rdk, dv, rdv))

    one, low, high, level = sums(grads)
    low, high, level = step(low, swap(high, YB), level)
    low, high, level = step(low, swap(high, YA), level)
    high, dk, dv = lax.optimization_barrier((high, dk, dv))
    got = swap(high, Z1)
    dk, dv = final(one, low, got, dk, dv)
    level = level + got[1:]
    level = level + lax.ppermute(level, "batch", [(0, 1), (1, 0)])
    level = level[0, 0].reshape(heads, HEAD)[:, :9].reshape(heads, 3, 3).sum(1).T
    return att[None], dq[None], dk[None], dv[None], level


def solution(mesh):
    rows = P("batch", "seq", None)
    return jax.shard_map(
        body,
        mesh=mesh,
        in_specs=(rows, rows, rows, rows, P()),
        out_specs=(rows, rows, rows, rows, P()),
        check_vma=False,
    )
```

```python
import functools
import math

import jax
import jax.numpy as jnp
from jax import lax
from jax.experimental import pallas as pl
from jax.experimental.pallas import tpu as pltpu
from jax.sharding import PartitionSpec as P

POOL1 = 16
POOL2 = 128
GROUP = 16
ROWS = 128
HEAD = 128
NEGATIVE = -1e30
LOG2E = math.log2(math.e)
LOG1 = math.log2(POOL1)
LOG2 = math.log2(POOL2)

SIB, Z1, YA, YB = 1, 16, 32, 96

BF = jnp.bfloat16
F32 = jnp.float32


def swap(x, mask):
    return lax.ppermute(x, "seq", [(i, i ^ mask) for i in range(lax.axis_size("seq"))])


def cross(x):
    size = lax.axis_size("seq")
    pairs = [(i, i + 1) for i in range(1, size - 1, 2)]
    return lax.ppermute(x, "seq", pairs + [(j, i) for i, j in pairs])


def in_group(x):
    size = lax.axis_size("seq")
    groups = [[g + i for i in range(GROUP)] for g in range(0, size, GROUP)]
    return lax.all_to_all(x, "seq", 0, 0, axis_index_groups=groups)


def params(limit=24):
    return pltpu.CompilerParams(vmem_limit_bytes=limit * 1024 * 1024)


def cost(us):
    return pl.CostEstimate(flops=0, bytes_accessed=int(us * 3.3e6), transcendentals=0)


def in_hbm(*arrays):
    return [pltpu.with_memory_space_constraint(x, pltpu.HBM) for x in arrays]


def out_hbm(shapes):
    return [pltpu.HBM(s.shape, s.dtype) for s in shapes]


def nt(a, b):
    return lax.dot_general(a, b, (((1,), (1,)), ((), ())), preferred_element_type=F32)


def nn(a, b):
    return lax.dot_general(a, b, (((1,), (0,)), ((), ())), preferred_element_type=F32)


def tn(a, b):
    return lax.dot_general(a, b, (((0,), (0,)), ((), ())), preferred_element_type=F32)


def pool_kernel(k_ref, v_ref, one_ref, two_ref):
    for n, ref in enumerate((k_ref, v_ref)):
        x = ref[...].astype(F32)
        sums = jnp.sum(x.reshape(ROWS // POOL1, POOL1, x.shape[-1]), axis=1)
        one_ref[8 * n : 8 * n + 8, :] = sums / POOL1
        row = jnp.sum(sums, axis=0, keepdims=True) / POOL2
        two_ref[0, n : n + 1, :] = row.astype(BF)


def pool(k, v):
    width = k.shape[1]
    return pl.pallas_call(
        pool_kernel,
        out_shape=(
            jax.ShapeDtypeStruct((16, width), F32),
            jax.ShapeDtypeStruct((1, 2, width), BF),
        ),
        compiler_params=params(),
        cost_estimate=cost(2),
    )(k, v)


def rows_kernel(one_ref, a_ref, b_ref, out_ref, far_ref):
    half = out_ref.shape[-1]
    for m, ref in enumerate((a_ref, b_ref)):
        for r in range(4):
            pair = ref[r].astype(F32)
            for n in range(2):
                to = 8 * n + 4 * m + r
                far_ref[to : to + 1, :] = pair[n : n + 1, :]
    for c in range(2):
        cols = slice(c * half, (c + 1) * half)
        one = one_ref[:, cols].astype(BF)
        far = far_ref[:, cols].astype(BF)
        for p in range(GROUP // 2):
            out_ref[2 * p + c, 0:16] = one
            out_ref[2 * p + c, 16:32] = far


def level_rows(one, a, b):
    width = one.shape[1]
    return pl.pallas_call(
        rows_kernel,
        out_shape=jax.ShapeDtypeStruct((GROUP, 32, width // 2), BF),
        scratch_shapes=[pltpu.VMEM((16, width), F32)],
        compiler_params=params(),
        cost_estimate=cost(1),
    )(one, a, b)


def prepare_kernel(ids_ref, *refs):
    arrays, wholes, halves, sems = refs[:4], refs[4:6], refs[6:10], refs[10]
    half = halves[0].shape[-1]
    start = pl.multiple_of((1 - ids_ref[1]) * half, half)
    copies = []
    for n, (ref, out) in enumerate(zip(arrays, halves)):
        part = ref.at[:, pl.ds(start, half)]
        copies.append(pltpu.make_async_copy(part, out, sems.at[n]))
    for n, ref in enumerate(arrays):
        to = wholes[n // 2].at[(n % 2) * ROWS : (n % 2 + 1) * ROWS]
        copies.append(pltpu.make_async_copy(ref, to, sems.at[4 + n]))
    for copy in copies:
        copy.start()
    for copy in copies:
        copy.wait()


def prepare(ids, *arrays):
    rows, width = arrays[0].shape
    smem = pl.BlockSpec(memory_space=pltpu.SMEM)
    hbm = pl.BlockSpec(memory_space=pltpu.HBM)
    return pl.pallas_call(
        prepare_kernel,
        in_specs=[smem] + [hbm] * 4,
        out_specs=[hbm] * 6,
        out_shape=[jax.ShapeDtypeStruct((2 * rows, width), BF)] * 2
        + [jax.ShapeDtypeStruct((rows, width // 2), BF)] * 4,
        scratch_shapes=[pltpu.SemaphoreType.DMA((8,))],
        compiler_params=params(),
        cost_estimate=cost(1),
    )(ids, *in_hbm(*arrays))


def other_kernel(ids_ref, x_ref, out_ref, sem):
    half = out_ref.shape[-1]
    start = pl.multiple_of((1 - ids_ref[1]) * half, half)
    copy = pltpu.make_async_copy(x_ref.at[:, pl.ds(start, half)], out_ref, sem)
    copy.start()
    copy.wait()


def other_half(ids, x):
    smem = pl.BlockSpec(memory_space=pltpu.SMEM)
    hbm = pl.BlockSpec(memory_space=pltpu.HBM)
    return pl.pallas_call(
        other_kernel,
        in_specs=[smem, hbm],
        out_specs=hbm,
        out_shape=jax.ShapeDtypeStruct((x.shape[0], x.shape[1] // 2), BF),
        scratch_shapes=[pltpu.SemaphoreType.DMA],
        compiler_params=params(),
        cost_estimate=cost(12),
    )(ids, x)


def split_rows(x):
    wide = x.astype(F32).reshape(GROUP, 16, HEAD)
    keys = wide[:, :8].reshape(ROWS, HEAD).astype(BF)
    return keys, wide[:, 8:].reshape(ROWS, HEAD).astype(BF)


def join_rows(a, b):
    both = [x.reshape(GROUP, 8, HEAD) for x in (a, b)]
    return jnp.concatenate(both, axis=1).astype(BF)


def pieces(sums):
    lane = lax.broadcasted_iota(jnp.int32, (1, HEAD), 1)
    row = jnp.zeros((1, HEAD), F32)
    for n, s in enumerate(sums):
        row = jnp.where(lane % 3 == n, jnp.sum(s, axis=1, keepdims=True), row)
    high = row.astype(BF).astype(F32)
    middle = (row - high).astype(BF).astype(F32)
    rest = row - high - middle
    row = jnp.where(lane < 3, high, jnp.where(lane < 6, middle, rest))
    return jnp.where(lane < 9, row, 0.0)


def attend_kernel(
    steps,
    heads,
    ids_ref,
    bias_ref,
    q_ref,
    k_ref,
    v_ref,
    c_ref,
    sq_ref,
    sk_ref,
    sv_ref,
    sc_ref,
    xk_ref,
    xv_ref,
    sxk_ref,
    sxv_ref,
    level_ref,
    att_ref,
    satt_ref,
    dq_ref,
    sdq_ref,
    dk_ref,
    dv_ref,
    sdk_ref,
    sdv_ref,
    glevel_ref,
    stat_ref,
    sstat_ref,
    mask_ref,
    edge_ref,
):
    step = pl.program_id(0)
    me, core = ids_ref[0], ids_ref[1]
    last = ids_ref[2] - 1
    scale = HEAD**-0.5
    unit = scale * LOG2E

    @pl.when(step == 0)
    def _():
        row = lax.broadcasted_iota(jnp.int32, (ROWS, 2 * ROWS), 0)
        lane = lax.broadcasted_iota(jnp.int32, (ROWS, 2 * ROWS), 1)
        block = jnp.where(lane < ROWS, me, me ^ 1)
        group = me // GROUP
        place, which = row // 8, row % 8
        good = jnp.abs(group * GROUP + place - block) >= 2
        mask_ref[0:ROWS] = jnp.where(good, LOG1, NEGATIVE)
        owner = (group ^ (which ^ ((which >> 2) << 1))) * GROUP + place
        good = (which != 0) & (jnp.abs(owner - block) >= 2)
        mask_ref[ROWS:] = jnp.where(good, LOG2, NEGATIVE)
        lane = lane[0:8]
        block = block[0:8]
        edge_ref[...] = jnp.where((block == 0) | (block == last), NEGATIVE, 0.0)

    def one_head(j):
        cols = slice(j * HEAD, (j + 1) * HEAD)
        head = step * heads + j
        whole_head = core * (steps * heads) + head
        bias = [bias_ref[n, whole_head] * LOG2E for n in range(3)]
        q, sq, c, sc = q_ref[:, cols], sq_ref[:, cols], c_ref[:, cols], sc_ref[:, cols]
        k_near = jnp.concatenate([k_ref[:, cols], sk_ref[:, cols]], axis=0)
        v_near = jnp.concatenate([v_ref[:, cols], sv_ref[:, cols]], axis=0)
        xk, xv, sxk, sxv = (
            ref[:, cols] for ref in (xk_ref, xv_ref, sxk_ref, sxv_ref)
        )
        k_one, v_one = split_rows(level_ref[:, 0:16, cols])
        k_two, v_two = split_rows(level_ref[:, 16:32, cols])
        k_far = jnp.concatenate([k_one, k_two], axis=0)
        v_far = jnp.concatenate([v_one, v_two], axis=0)
        q_both = jnp.concatenate([q, sq], axis=0)
        c_both = jnp.concatenate([c, sc], axis=0)

        near = nt(k_near, q_both)
        edge = jnp.concatenate([nt(xk, q), nt(sxk, sq)], axis=1)
        far = nt(k_far, q_both) * unit + mask_ref[...]
        yield
        parts = [near, edge, far[0:ROWS], far[ROWS:]]
        shifts = [bias[0], bias[0] + edge_ref[0:1], bias[1], bias[2]]
        tops = [jnp.max(x, axis=0, keepdims=True) for x in parts]
        tops = [t * unit for t in tops[:2]] + tops[2:]
        top = functools.reduce(jnp.maximum, [t + s for t, s in zip(tops, shifts)])
        parts = [x * unit for x in parts[:2]] + parts[2:]
        powers = [jnp.exp2(x + (s - top)) for x, s in zip(parts, shifts)]
        masses = [jnp.sum(p, axis=0, keepdims=True) for p in powers]
        total = sum(masses)
        share = 1.0 / total
        weights = [p * share for p in powers]

        yield
        g_far = nt(v_far, c_both)
        grads = [
            nt(v_near, c_both),
            jnp.concatenate([nt(xv, c), nt(sxv, sc)], axis=1),
            g_far[0:ROWS],
            g_far[ROWS:],
        ]
        yield
        deltas = [
            jnp.sum(w * g, axis=0, keepdims=True) for w, g in zip(weights, grads)
        ]
        delta = sum(deltas)
        score_grads = [w * (g - delta) for w, g in zip(weights, grads)]
        w_near, w_edge, w_one, w_two = [w.astype(BF) for w in weights]
        d_near, d_edge, d_one, d_two = [d.astype(BF) for d in score_grads]
        yield
        w_far = jnp.concatenate([w_one, w_two], axis=0)
        d_far = jnp.concatenate([d_one, d_two], axis=0)

        att = tn(w_near, v_near) + tn(w_far, v_far)
        att_ref[:, cols] = (att[0:ROWS] + tn(w_edge[:, 0:ROWS], xv)).astype(BF)
        satt_ref[:, cols] = (att[ROWS:] + tn(w_edge[:, ROWS:], sxv)).astype(BF)
        dq = tn(d_near, k_near) + tn(d_far, k_far)
        dq_ref[:, cols] = ((dq[0:ROWS] + tn(d_edge[:, 0:ROWS], xk)) * scale).astype(BF)
        sdq_ref[:, cols] = ((dq[ROWS:] + tn(d_edge[:, ROWS:], sxk)) * scale).astype(BF)

        yield
        dk = nn(d_near, q_both) * scale
        dk_ref[:, cols] = dk[0:ROWS]
        sdk_ref[:, cols] = dk[ROWS:]
        dv = nn(w_near, c_both)
        dv_ref[:, cols] = dv[0:ROWS]
        sdv_ref[:, cols] = dv[ROWS:]
        dk = nn(d_far, q_both) * scale
        dv = nn(w_far, c_both)
        glevel_ref[:, 0:16, cols] = join_rows(dk[0:ROWS], dv[0:ROWS])
        loads = [d - m * (share * delta) for d, m in zip(deltas, masses)]
        level = pieces([loads[0] + loads[1], loads[2], loads[3]])
        first = lax.broadcasted_iota(jnp.int32, (ROWS, HEAD), 0) % 8 == 0
        glevel_ref[:, 16:32, cols] = join_rows(
            jnp.where(first, level, dk[ROWS:]), dv[ROWS:]
        )

        log_total = top + jnp.log(total) * LOG2E
        row = pl.ds(head, 1)
        low = pl.ds(head + 8, 1)
        stat_ref[row] = log_total[:, 0:ROWS]
        sstat_ref[row] = log_total[:, ROWS:]
        stat_ref[low] = delta[:, 0:ROWS]
        sstat_ref[low] = delta[:, ROWS:]

    running = [one_head(j) for j in range(heads)]
    for turn in range(heads + 5):
        for j in range(heads):
            if 0 <= turn - j <= 5:
                next(running[j], None)


def attend(ids, bias, own, sib, x, sx, level):
    width = own[0].shape[1]
    half = width // 2
    heads = 4
    block = heads * HEAD
    steps = half // block
    rows = ROWS

    def mine(n, at=0):
        return pl.BlockSpec((n, block), lambda i, ids: (at, ids[1] * steps + i))

    def part(n, at=0):
        return pl.BlockSpec((n, block), lambda i, ids: (at, i))

    rows_of = pl.BlockSpec((GROUP, 32, block), lambda i, ids: (0, 0, i))
    stat = pl.BlockSpec((16, rows), lambda i, ids: (0, 0))
    low = jax.ShapeDtypeStruct((rows, half), BF)
    high = jax.ShapeDtypeStruct((rows, half), F32)
    stats = jax.ShapeDtypeStruct((16, rows), F32)
    return pl.pallas_call(
        functools.partial(attend_kernel, steps, heads),
        grid_spec=pltpu.PrefetchScalarGridSpec(
            num_scalar_prefetch=1,
            grid=(steps,),
            in_specs=[pl.BlockSpec(memory_space=pltpu.SMEM)]
            + [mine(rows)] * 4
            + [part(rows)] * 4
            + [mine(rows), mine(rows, 1), part(rows), part(rows, 1)]
            + [rows_of],
            out_specs=[part(rows)] * 8 + [rows_of] + [stat] * 2,
            scratch_shapes=[
                pltpu.VMEM((2 * rows, 2 * rows), F32),
                pltpu.VMEM((8, 2 * rows), F32),
            ],
        ),
        out_shape=out_hbm(
            [low] * 4
            + [high] * 4
            + [jax.ShapeDtypeStruct((GROUP, 32, half), BF)]
            + [stats] * 2
        ),
        compiler_params=params(),
        cost_estimate=cost(9),
    )(ids, bias, *in_hbm(*own, *sib, x, x, sx, sx), level)


def edge_kernel(
    half,
    heads,
    ids_ref,
    bias_ref,
    k_ref,
    v_ref,
    q_ref,
    c_ref,
    stat_ref,
    dk_ref,
    sdk_ref,
    dv_ref,
    sdv_ref,
    out_dk_ref,
    out_dv_ref,
):
    step = pl.program_id(0)
    mine = half == ids_ref[1]
    scale = HEAD**-0.5
    for j in range(heads):
        cols = slice(j * HEAD, (j + 1) * HEAD)
        bias = bias_ref[0, half * 8 + step * heads + j] * LOG2E
        row = step * heads + j
        log_total = stat_ref[0, pl.ds(row, 1)]
        delta = stat_ref[0, pl.ds(row + 8, 1)]
        q, c = q_ref[:, cols], c_ref[:, cols]
        score = nt(k_ref[:, cols], q) * (scale * LOG2E)
        weights = jnp.exp2(score + (bias - log_total))
        score_grad = weights * (nt(v_ref[:, cols], c) - delta)
        dk = jnp.where(mine, dk_ref[:, cols], sdk_ref[:, cols])
        dv = jnp.where(mine, dv_ref[:, cols], sdv_ref[:, cols])
        out_dk_ref[:, cols] = dk + nn(score_grad.astype(BF), q) * scale
        out_dv_ref[:, cols] = dv + nn(weights.astype(BF), c)


def edge(half, ids, bias, k, v, x, stat, parts):
    rows, width = k.shape
    heads = 4
    block = heads * HEAD
    per_half = width // 2 // block
    whole = pl.BlockSpec((rows, block), lambda i, ids: (0, half * per_half + i))
    part = pl.BlockSpec((rows, block), lambda i, ids: (0, i))
    return pl.pallas_call(
        functools.partial(edge_kernel, half, heads),
        grid_spec=pltpu.PrefetchScalarGridSpec(
            num_scalar_prefetch=1,
            grid=(per_half,),
            in_specs=[
                pl.BlockSpec(memory_space=pltpu.SMEM),
                whole,
                whole,
                whole,
                pl.BlockSpec((rows, block), lambda i, ids: (1, half * per_half + i)),
                pl.BlockSpec((1, 16, rows), lambda i, ids: (half, 0, 0)),
            ]
            + [part] * 4,
            out_specs=[part] * 2,
        ),
        out_shape=[jax.ShapeDtypeStruct((rows, width // 2), F32)] * 2,
        compiler_params=params(),
        cost_estimate=cost(5),
    )(ids, bias, *in_hbm(k, v), x, x, *in_hbm(stat, *parts))


def join_kernel(ids_ref, att_ref, satt_ref, dq_ref, sdq_ref, out_att_ref, out_dq_ref):
    mine = pl.program_id(0) == ids_ref[1]
    out_att_ref[...] = jnp.where(mine, att_ref[...], satt_ref[...])
    out_dq_ref[...] = jnp.where(mine, dq_ref[...], sdq_ref[...])


def join(ids, *parts):
    rows, half = parts[0].shape
    part = pl.BlockSpec((rows, half), lambda i, ids: (0, 0))
    return pl.pallas_call(
        join_kernel,
        grid_spec=pltpu.PrefetchScalarGridSpec(
            num_scalar_prefetch=1,
            grid=(2,),
            in_specs=[part] * 4,
            out_specs=[pl.BlockSpec((rows, half), lambda i, ids: (0, i))] * 2,
        ),
        out_shape=out_hbm([jax.ShapeDtypeStruct((rows, 2 * half), BF)] * 2),
        compiler_params=params(),
        cost_estimate=cost(6),
    )(ids, *in_hbm(*parts))


def sums_kernel(x_ref, one_ref, low_ref, high_ref, level_ref):
    total = jnp.sum(x_ref[:, 0].astype(F32), axis=0)
    one_ref[...] = total[0:16]
    zero = jnp.zeros((1, total.shape[-1]), F32)
    for n in range(2):
        at = 16 + 8 * n
        for r in range(4):
            row = total[at + r : at + r + 1]
            low_ref[r, n : n + 1, :] = row if r else zero
            high_ref[r, n : n + 1, :] = total[at + 4 + r : at + 5 + r]
        row = total[at : at + 1]
        high_ref[4, n : n + 1, :] = row
        level_ref[0, n : n + 1, :] = row


def sums(x):
    half = x.shape[-1]
    block = 512
    per_half = half // block
    x = x.reshape(GROUP // 2, 2, 32, half)
    return pl.pallas_call(
        sums_kernel,
        grid=(2 * per_half,),
        in_specs=[
            pl.BlockSpec(
                (GROUP // 2, 1, 32, block),
                lambda i: (0, i // per_half, 0, lax.rem(i, per_half)),
            )
        ],
        out_specs=[pl.BlockSpec((16, block), lambda i: (0, i))]
        + [pl.BlockSpec((n, 2, block), lambda i: (0, 0, i)) for n in (4, 5, 1)],
        out_shape=[jax.ShapeDtypeStruct((16, 2 * half), F32)]
        + [jax.ShapeDtypeStruct((n, 2, 2 * half), F32) for n in (4, 5, 1)],
        compiler_params=params(),
        cost_estimate=cost(1),
    )(x)


def step_kernel(low_ref, got_ref, level_ref, out_low_ref, out_high_ref, out_level_ref):
    count = low_ref.shape[0]
    half = count // 2
    out_low_ref[...] = low_ref[0:half] + got_ref[0:half]
    out_high_ref[0:half] = low_ref[half:count] + got_ref[half:count]
    level = level_ref[...] + got_ref[count:]
    out_level_ref[...] = level
    out_high_ref[half:] = level


def step(low, got, level):
    half, width = low.shape[0] // 2, low.shape[2]
    counts = (half, half + 1, 1)
    return pl.pallas_call(
        step_kernel,
        out_shape=[jax.ShapeDtypeStruct((n, 2, width), F32) for n in counts],
        compiler_params=params(),
        cost_estimate=cost(1),
    )(low, got, level)


def final_kernel(
    one_ref, far_ref, got_ref, dk_ref, dv_ref, dk2_ref, dv2_ref, out_dk_ref, out_dv_ref
):
    lower = pl.program_id(0) < pl.num_programs(0) // 2
    total = one_ref[...] / POOL1
    triples = (dk_ref, dk2_ref, out_dk_ref), (dv_ref, dv2_ref, out_dv_ref)
    for n, (ref, ref2, out) in enumerate(triples):
        far = far_ref[0, n : n + 1, :] + got_ref[0, n : n + 1, :]
        rows = total[8 * n : 8 * n + 8] + far / POOL2
        for r in range(8):
            at = slice(r * POOL1, (r + 1) * POOL1)
            near = jnp.where(lower, ref[at], ref2[at])
            out[at] = (near + rows[r : r + 1]).astype(BF)


def final(one, far, got, *nears):
    rows, width = nears[0].shape[0], one.shape[1]
    block = 512
    steps = width // block
    whole = pl.BlockSpec((rows, block), lambda i: (0, i))
    return pl.pallas_call(
        final_kernel,
        grid=(steps,),
        in_specs=[
            pl.BlockSpec((16, block), lambda i: (0, i)),
            pl.BlockSpec((1, 2, block), lambda i: (0, 0, i)),
            pl.BlockSpec((2, 2, block), lambda i: (0, 0, i)),
        ]
        + [pl.BlockSpec((rows, block), lambda i: (0, lax.rem(i, steps // 2)))] * 4,
        out_specs=[whole] * 2,
        out_shape=[jax.ShapeDtypeStruct((rows, width), BF)] * 2,
        compiler_params=params(),
        cost_estimate=cost(2),
    )(one, far, got, *nears)


def body(queries, key_rows, values, cotangent, level_bias):
    q, k, v, c = queries[0], key_rows[0], values[0], cotangent[0]
    heads = level_bias.shape[1]
    size = lax.axis_size("seq")
    me = lax.axis_index("seq")
    core = me % 2
    ids = jnp.stack([me, core, size]).astype(jnp.int32)

    kv, qc, *sends = prepare(ids, k, v, q, c)
    x = cross(kv)
    one, far = pool(k, v)
    far = jnp.concatenate([far, swap(far, Z1)], axis=0)
    far = jnp.concatenate([far, swap(far, YA)], axis=0)
    rows = level_rows(one, far, swap(far, YB))

    sk, sv, sq, sc = [swap(s, SIB) for s in sends]
    rows, x, sk, sv, sq, sc = lax.optimization_barrier((rows, x, sk, sv, sq, sc))
    rows = in_group(rows)
    sx = swap(other_half(ids, x), SIB)
    late, rows, sx = lax.optimization_barrier((qc, rows, sx))
    x_qc = cross(late)

    att, satt, dq, sdq, dk, dv, sdk, sdv, grads, stat, sstat = attend(
        ids, level_bias, (q, k, v, c), (sq, sk, sv, sc), x, sx, rows
    )

    grads, x_qc = lax.optimization_barrier((grads, x_qc))
    grads = in_group(grads)

    rstat = swap(sstat, SIB)
    stats = jnp.where(core == 0, jnp.stack([stat, rstat]), jnp.stack([rstat, stat]))
    x_stats = cross(stats)
    grads, x_stats = lax.optimization_barrier((grads, x_stats))
    ratt, rdq, rdk, rdv = [swap(s, SIB) for s in (satt, sdq, sdk, sdv)]
    att, dq = join(ids, att, ratt, dq, rdq)
    grads, att, dq = lax.optimization_barrier((grads, att, dq))
    first, second = [
        edge(half, ids, level_bias, k, v, x_qc, x_stats, (dk, rdk, dv, rdv))
        for half in range(2)
    ]

    one, low, high, level = sums(grads)
    low, high, level = step(low, swap(high, YB), level)
    high, first = lax.optimization_barrier((high, first))
    low, high, level = step(low, swap(high, YA), level)
    high, second = lax.optimization_barrier((high, second))
    got = swap(high, Z1)
    dk, dv = final(one, low, got, *first, *second)
    level = level + got[1:]
    level = level + lax.ppermute(level, "batch", [(0, 1), (1, 0)])
    level = level[0, 0].reshape(heads, HEAD)[:, :9].reshape(heads, 3, 3).sum(1).T
    return att[None], dq[None], dk[None], dv[None], level


def solution(mesh):
    rows = P("batch", "seq", None)
    return jax.shard_map(
        body,
        mesh=mesh,
        in_specs=(rows, rows, rows, rows, P()),
        out_specs=(rows, rows, rows, rows, P()),
        check_vma=False,
    )
```

```python
import functools
import math

import jax
import jax.numpy as jnp
from jax import lax
from jax.experimental import pallas as pl
from jax.experimental.pallas import tpu as pltpu
from jax.sharding import PartitionSpec as P

POOL1 = 16
POOL2 = 128
GROUP = 16
ROWS = 128
HEAD = 128
NEGATIVE = -1e30
LOG2E = math.log2(math.e)
LOG1 = math.log2(POOL1)
LOG2 = math.log2(POOL2)

SIB, Z1, YA, YB = 1, 16, 32, 96

BF = jnp.bfloat16
F32 = jnp.float32


def swap(x, mask):
    return lax.ppermute(x, "seq", [(i, i ^ mask) for i in range(lax.axis_size("seq"))])


def cross(x):
    size = lax.axis_size("seq")
    pairs = [(i, i + 1) for i in range(1, size - 1, 2)]
    return lax.ppermute(x, "seq", pairs + [(j, i) for i, j in pairs])


def in_group(x):
    size = lax.axis_size("seq")
    groups = [[g + i for i in range(GROUP)] for g in range(0, size, GROUP)]
    return lax.all_to_all(x, "seq", 0, 0, axis_index_groups=groups)


def params(limit=24):
    return pltpu.CompilerParams(vmem_limit_bytes=limit * 1024 * 1024)


def cost(us):
    return pl.CostEstimate(flops=0, bytes_accessed=int(us * 3.3e6), transcendentals=0)


def in_hbm(*arrays):
    return [pltpu.with_memory_space_constraint(x, pltpu.HBM) for x in arrays]


def out_hbm(shapes):
    return [pltpu.HBM(s.shape, s.dtype) for s in shapes]


def nt(a, b):
    return lax.dot_general(a, b, (((1,), (1,)), ((), ())), preferred_element_type=F32)


def nn(a, b):
    return lax.dot_general(a, b, (((1,), (0,)), ((), ())), preferred_element_type=F32)


def tn(a, b):
    return lax.dot_general(a, b, (((0,), (0,)), ((), ())), preferred_element_type=F32)


def pool_kernel(k_ref, v_ref, one_ref, two_ref):
    for n, ref in enumerate((k_ref, v_ref)):
        x = ref[...].astype(F32)
        sums = jnp.sum(x.reshape(ROWS // POOL1, POOL1, x.shape[-1]), axis=1)
        one_ref[8 * n : 8 * n + 8, :] = sums / POOL1
        row = jnp.sum(sums, axis=0, keepdims=True) / POOL2
        two_ref[0, n : n + 1, :] = row.astype(BF)


def pool(k, v):
    width = k.shape[1]
    return pl.pallas_call(
        pool_kernel,
        out_shape=(
            jax.ShapeDtypeStruct((16, width), F32),
            jax.ShapeDtypeStruct((1, 2, width), BF),
        ),
        compiler_params=params(),
        cost_estimate=cost(2),
    )(k, v)


def rows_kernel(one_ref, a_ref, b_ref, out_ref, far_ref):
    half = out_ref.shape[-1]
    for m, ref in enumerate((a_ref, b_ref)):
        for r in range(4):
            pair = ref[r].astype(F32)
            for n in range(2):
                to = 8 * n + 4 * m + r
                far_ref[to : to + 1, :] = pair[n : n + 1, :]
    for c in range(2):
        cols = slice(c * half, (c + 1) * half)
        one = one_ref[:, cols].astype(BF)
        far = far_ref[:, cols].astype(BF)
        for p in range(GROUP // 2):
            out_ref[2 * p + c, 0:16] = one
            out_ref[2 * p + c, 16:32] = far


def level_rows(one, a, b):
    width = one.shape[1]
    return pl.pallas_call(
        rows_kernel,
        out_shape=jax.ShapeDtypeStruct((GROUP, 32, width // 2), BF),
        scratch_shapes=[pltpu.VMEM((16, width), F32)],
        compiler_params=params(),
        cost_estimate=cost(1),
    )(one, a, b)


def prepare_kernel(ids_ref, *refs):
    arrays, wholes, halves, sems = refs[:4], refs[4:6], refs[6:10], refs[10]
    half = halves[0].shape[-1]
    start = pl.multiple_of((1 - ids_ref[1]) * half, half)
    copies = []
    for n, (ref, out) in enumerate(zip(arrays, halves)):
        part = ref.at[:, pl.ds(start, half)]
        copies.append(pltpu.make_async_copy(part, out, sems.at[n]))
    for n, ref in enumerate(arrays):
        to = wholes[n // 2].at[(n % 2) * ROWS : (n % 2 + 1) * ROWS]
        copies.append(pltpu.make_async_copy(ref, to, sems.at[4 + n]))
    for copy in copies:
        copy.start()
    for copy in copies:
        copy.wait()


def prepare(ids, *arrays):
    rows, width = arrays[0].shape
    smem = pl.BlockSpec(memory_space=pltpu.SMEM)
    hbm = pl.BlockSpec(memory_space=pltpu.HBM)
    return pl.pallas_call(
        prepare_kernel,
        in_specs=[smem] + [hbm] * 4,
        out_specs=[hbm] * 6,
        out_shape=[jax.ShapeDtypeStruct((2 * rows, width), BF)] * 2
        + [jax.ShapeDtypeStruct((rows, width // 2), BF)] * 4,
        scratch_shapes=[pltpu.SemaphoreType.DMA((8,))],
        compiler_params=params(),
        cost_estimate=cost(1),
    )(ids, *in_hbm(*arrays))


def other_kernel(ids_ref, x_ref, out_ref, sem):
    half = out_ref.shape[-1]
    start = pl.multiple_of((1 - ids_ref[1]) * half, half)
    copy = pltpu.make_async_copy(x_ref.at[:, pl.ds(start, half)], out_ref, sem)
    copy.start()
    copy.wait()


def other_half(ids, x):
    smem = pl.BlockSpec(memory_space=pltpu.SMEM)
    hbm = pl.BlockSpec(memory_space=pltpu.HBM)
    return pl.pallas_call(
        other_kernel,
        in_specs=[smem, hbm],
        out_specs=hbm,
        out_shape=jax.ShapeDtypeStruct((x.shape[0], x.shape[1] // 2), BF),
        scratch_shapes=[pltpu.SemaphoreType.DMA],
        compiler_params=params(),
        cost_estimate=cost(12),
    )(ids, x)


def split_rows(x):
    wide = x.astype(F32).reshape(GROUP, 16, HEAD)
    keys = wide[:, :8].reshape(ROWS, HEAD).astype(BF)
    return keys, wide[:, 8:].reshape(ROWS, HEAD).astype(BF)


def join_rows(a, b):
    both = [x.reshape(GROUP, 8, HEAD) for x in (a, b)]
    return jnp.concatenate(both, axis=1).astype(BF)


def pieces(sums):
    lane = lax.broadcasted_iota(jnp.int32, (1, HEAD), 1)
    row = jnp.zeros((1, HEAD), F32)
    for n, s in enumerate(sums):
        row = jnp.where(lane % 3 == n, jnp.sum(s, axis=1, keepdims=True), row)
    high = row.astype(BF).astype(F32)
    middle = (row - high).astype(BF).astype(F32)
    rest = row - high - middle
    row = jnp.where(lane < 3, high, jnp.where(lane < 6, middle, rest))
    return jnp.where(lane < 9, row, 0.0)


def attend_kernel(
    steps,
    heads,
    ids_ref,
    bias_ref,
    q_ref,
    k_ref,
    v_ref,
    c_ref,
    sq_ref,
    sk_ref,
    sv_ref,
    sc_ref,
    xk_ref,
    xv_ref,
    sxk_ref,
    sxv_ref,
    level_ref,
    att_ref,
    satt_ref,
    dq_ref,
    sdq_ref,
    dk_ref,
    dv_ref,
    sdk_ref,
    sdv_ref,
    glevel_ref,
    stat_ref,
    sstat_ref,
    mask_ref,
    edge_ref,
):
    step = pl.program_id(0)
    me, core = ids_ref[0], ids_ref[1]
    last = ids_ref[2] - 1
    scale = HEAD**-0.5
    unit = scale * LOG2E

    @pl.when(step == 0)
    def _():
        row = lax.broadcasted_iota(jnp.int32, (ROWS, 2 * ROWS), 0)
        lane = lax.broadcasted_iota(jnp.int32, (ROWS, 2 * ROWS), 1)
        block = jnp.where(lane < ROWS, me, me ^ 1)
        group = me // GROUP
        place, which = row // 8, row % 8
        good = jnp.abs(group * GROUP + place - block) >= 2
        mask_ref[0:ROWS] = jnp.where(good, LOG1, NEGATIVE)
        owner = (group ^ (which ^ ((which >> 2) << 1))) * GROUP + place
        good = (which != 0) & (jnp.abs(owner - block) >= 2)
        mask_ref[ROWS:] = jnp.where(good, LOG2, NEGATIVE)
        lane = lane[0:8]
        block = block[0:8]
        edge_ref[...] = jnp.where((block == 0) | (block == last), NEGATIVE, 0.0)

    def one_head(j):
        cols = slice(j * HEAD, (j + 1) * HEAD)
        head = step * heads + j
        whole_head = core * (steps * heads) + head
        bias = [bias_ref[n, whole_head] * LOG2E for n in range(3)]
        q, sq, c, sc = q_ref[:, cols], sq_ref[:, cols], c_ref[:, cols], sc_ref[:, cols]
        k_near = jnp.concatenate([k_ref[:, cols], sk_ref[:, cols]], axis=0)
        v_near = jnp.concatenate([v_ref[:, cols], sv_ref[:, cols]], axis=0)
        xk, xv, sxk, sxv = (
            ref[:, cols] for ref in (xk_ref, xv_ref, sxk_ref, sxv_ref)
        )
        k_one, v_one = split_rows(level_ref[:, 0:16, cols])
        k_two, v_two = split_rows(level_ref[:, 16:32, cols])
        k_far = jnp.concatenate([k_one, k_two], axis=0)
        v_far = jnp.concatenate([v_one, v_two], axis=0)
        q_both = jnp.concatenate([q, sq], axis=0)
        c_both = jnp.concatenate([c, sc], axis=0)

        near = nt(k_near, q_both)
        edge = jnp.concatenate([nt(xk, q), nt(sxk, sq)], axis=1)
        far = nt(k_far, q_both) * unit + mask_ref[...]
        yield
        parts = [near, edge, far[0:ROWS], far[ROWS:]]
        shifts = [bias[0], bias[0] + edge_ref[0:1], bias[1], bias[2]]
        tops = [jnp.max(x, axis=0, keepdims=True) for x in parts]
        tops = [t * unit for t in tops[:2]] + tops[2:]
        top = functools.reduce(jnp.maximum, [t + s for t, s in zip(tops, shifts)])
        parts = [x * unit for x in parts[:2]] + parts[2:]
        powers = [jnp.exp2(x + (s - top)) for x, s in zip(parts, shifts)]
        masses = [jnp.sum(p, axis=0, keepdims=True) for p in powers]
        total = sum(masses)
        share = 1.0 / total
        weights = [p * share for p in powers]

        yield
        g_far = nt(v_far, c_both)
        grads = [
            nt(v_near, c_both),
            jnp.concatenate([nt(xv, c), nt(sxv, sc)], axis=1),
            g_far[0:ROWS],
            g_far[ROWS:],
        ]
        yield
        deltas = [
            jnp.sum(w * g, axis=0, keepdims=True) for w, g in zip(weights, grads)
        ]
        delta = sum(deltas)
        score_grads = [w * (g - delta) for w, g in zip(weights, grads)]
        w_near, w_edge, w_one, w_two = [w.astype(BF) for w in weights]
        d_near, d_edge, d_one, d_two = [d.astype(BF) for d in score_grads]
        yield
        w_far = jnp.concatenate([w_one, w_two], axis=0)
        d_far = jnp.concatenate([d_one, d_two], axis=0)

        att = tn(w_near, v_near) + tn(w_far, v_far)
        att_ref[:, cols] = (att[0:ROWS] + tn(w_edge[:, 0:ROWS], xv)).astype(BF)
        satt_ref[:, cols] = (att[ROWS:] + tn(w_edge[:, ROWS:], sxv)).astype(BF)
        dq = tn(d_near, k_near) + tn(d_far, k_far)
        dq_ref[:, cols] = ((dq[0:ROWS] + tn(d_edge[:, 0:ROWS], xk)) * scale).astype(BF)
        sdq_ref[:, cols] = ((dq[ROWS:] + tn(d_edge[:, ROWS:], sxk)) * scale).astype(BF)

        yield
        dk = nn(d_near, q_both) * scale
        dk_ref[:, cols] = dk[0:ROWS]
        sdk_ref[:, cols] = dk[ROWS:]
        dv = nn(w_near, c_both)
        dv_ref[:, cols] = dv[0:ROWS]
        sdv_ref[:, cols] = dv[ROWS:]
        dk = nn(d_far, q_both) * scale
        dv = nn(w_far, c_both)
        glevel_ref[:, 0:16, cols] = join_rows(dk[0:ROWS], dv[0:ROWS])
        loads = [d - m * (share * delta) for d, m in zip(deltas, masses)]
        level = pieces([loads[0] + loads[1], loads[2], loads[3]])
        first = lax.broadcasted_iota(jnp.int32, (ROWS, HEAD), 0) % 8 == 0
        glevel_ref[:, 16:32, cols] = join_rows(
            jnp.where(first, level, dk[ROWS:]), dv[ROWS:]
        )

        log_total = top + jnp.log(total) * LOG2E
        row = pl.ds(head, 1)
        low = pl.ds(head + 8, 1)
        stat_ref[row] = log_total[:, 0:ROWS]
        sstat_ref[row] = log_total[:, ROWS:]
        stat_ref[low] = delta[:, 0:ROWS]
        sstat_ref[low] = delta[:, ROWS:]

    running = [one_head(j) for j in range(heads)]
    for turn in range(heads + 5):
        for j in range(heads):
            if 0 <= turn - j <= 5:
                next(running[j], None)


def attend(ids, bias, own, sib, x, sx, level):
    width = own[0].shape[1]
    half = width // 2
    heads = 4
    block = heads * HEAD
    steps = half // block
    rows = ROWS

    def mine(n, at=0):
        return pl.BlockSpec((n, block), lambda i, ids: (at, ids[1] * steps + i))

    def part(n, at=0):
        return pl.BlockSpec((n, block), lambda i, ids: (at, i))

    rows_of = pl.BlockSpec((GROUP, 32, block), lambda i, ids: (0, 0, i))
    stat = pl.BlockSpec((16, rows), lambda i, ids: (0, 0))
    low = jax.ShapeDtypeStruct((rows, half), BF)
    high = jax.ShapeDtypeStruct((rows, half), F32)
    stats = jax.ShapeDtypeStruct((16, rows), F32)
    return pl.pallas_call(
        functools.partial(attend_kernel, steps, heads),
        grid_spec=pltpu.PrefetchScalarGridSpec(
            num_scalar_prefetch=1,
            grid=(steps,),
            in_specs=[pl.BlockSpec(memory_space=pltpu.SMEM)]
            + [mine(rows)] * 4
            + [part(rows)] * 4
            + [mine(rows), mine(rows, 1), part(rows), part(rows, 1)]
            + [rows_of],
            out_specs=[part(rows)] * 8 + [rows_of] + [stat] * 2,
            scratch_shapes=[
                pltpu.VMEM((2 * rows, 2 * rows), F32),
                pltpu.VMEM((8, 2 * rows), F32),
            ],
        ),
        out_shape=out_hbm(
            [low] * 4
            + [high] * 4
            + [jax.ShapeDtypeStruct((GROUP, 32, half), BF)]
            + [stats] * 2
        ),
        compiler_params=params(),
        cost_estimate=cost(9),
    )(ids, bias, *in_hbm(*own, *sib, x, x, sx, sx), level)


def edge_kernel(
    half,
    heads,
    ids_ref,
    bias_ref,
    k_ref,
    v_ref,
    q_ref,
    c_ref,
    stat_ref,
    dk_ref,
    sdk_ref,
    dv_ref,
    sdv_ref,
    out_dk_ref,
    out_dv_ref,
):
    step = pl.program_id(0)
    mine = half == ids_ref[1]
    scale = HEAD**-0.5
    for j in range(heads):
        cols = slice(j * HEAD, (j + 1) * HEAD)
        bias = bias_ref[0, half * 8 + step * heads + j] * LOG2E
        row = step * heads + j
        log_total = stat_ref[0, pl.ds(row, 1)]
        delta = stat_ref[0, pl.ds(row + 8, 1)]
        q, c = q_ref[:, cols], c_ref[:, cols]
        score = nt(k_ref[:, cols], q) * (scale * LOG2E)
        weights = jnp.exp2(score + (bias - log_total))
        score_grad = weights * (nt(v_ref[:, cols], c) - delta)
        dk = jnp.where(mine, dk_ref[:, cols], sdk_ref[:, cols])
        dv = jnp.where(mine, dv_ref[:, cols], sdv_ref[:, cols])
        out_dk_ref[:, cols] = dk + nn(score_grad.astype(BF), q) * scale
        out_dv_ref[:, cols] = dv + nn(weights.astype(BF), c)


def edge(half, ids, bias, k, v, x, stat, parts):
    rows, width = k.shape
    heads = 4
    block = heads * HEAD
    per_half = width // 2 // block
    whole = pl.BlockSpec((rows, block), lambda i, ids: (0, half * per_half + i))
    part = pl.BlockSpec((rows, block), lambda i, ids: (0, i))
    return pl.pallas_call(
        functools.partial(edge_kernel, half, heads),
        grid_spec=pltpu.PrefetchScalarGridSpec(
            num_scalar_prefetch=1,
            grid=(per_half,),
            in_specs=[
                pl.BlockSpec(memory_space=pltpu.SMEM),
                whole,
                whole,
                whole,
                pl.BlockSpec((rows, block), lambda i, ids: (1, half * per_half + i)),
                pl.BlockSpec((1, 16, rows), lambda i, ids: (half, 0, 0)),
            ]
            + [part] * 4,
            out_specs=[part] * 2,
        ),
        out_shape=[jax.ShapeDtypeStruct((rows, width // 2), F32)] * 2,
        compiler_params=params(),
        cost_estimate=cost(5),
    )(ids, bias, *in_hbm(k, v), x, x, *in_hbm(stat, *parts))


def join_kernel(ids_ref, att_ref, satt_ref, dq_ref, sdq_ref, out_att_ref, out_dq_ref):
    mine = pl.program_id(0) == ids_ref[1]
    out_att_ref[...] = jnp.where(mine, att_ref[...], satt_ref[...])
    out_dq_ref[...] = jnp.where(mine, dq_ref[...], sdq_ref[...])


def join(ids, *parts):
    rows, half = parts[0].shape
    part = pl.BlockSpec((rows, half), lambda i, ids: (0, 0))
    return pl.pallas_call(
        join_kernel,
        grid_spec=pltpu.PrefetchScalarGridSpec(
            num_scalar_prefetch=1,
            grid=(2,),
            in_specs=[part] * 4,
            out_specs=[pl.BlockSpec((rows, half), lambda i, ids: (0, i))] * 2,
        ),
        out_shape=out_hbm([jax.ShapeDtypeStruct((rows, 2 * half), BF)] * 2),
        compiler_params=params(),
        cost_estimate=cost(6),
    )(ids, *in_hbm(*parts))


def sums_kernel(x_ref, one_ref, low_ref, high_ref, level_ref):
    total = jnp.sum(x_ref[:, 0].astype(F32), axis=0)
    one_ref[...] = total[0:16]
    zero = jnp.zeros((1, total.shape[-1]), F32)
    for n in range(2):
        at = 16 + 8 * n
        for r in range(4):
            row = total[at + r : at + r + 1]
            low_ref[r, n : n + 1, :] = row if r else zero
            high_ref[r, n : n + 1, :] = total[at + 4 + r : at + 5 + r]
        row = total[at : at + 1]
        high_ref[4, n : n + 1, :] = row
        level_ref[0, n : n + 1, :] = row


def sums(x):
    half = x.shape[-1]
    block = 512
    per_half = half // block
    x = x.reshape(GROUP // 2, 2, 32, half)
    return pl.pallas_call(
        sums_kernel,
        grid=(2 * per_half,),
        in_specs=[
            pl.BlockSpec(
                (GROUP // 2, 1, 32, block),
                lambda i: (0, i // per_half, 0, lax.rem(i, per_half)),
            )
        ],
        out_specs=[pl.BlockSpec((16, block), lambda i: (0, i))]
        + [pl.BlockSpec((n, 2, block), lambda i: (0, 0, i)) for n in (4, 5, 1)],
        out_shape=[jax.ShapeDtypeStruct((16, 2 * half), F32)]
        + [jax.ShapeDtypeStruct((n, 2, 2 * half), F32) for n in (4, 5, 1)],
        compiler_params=params(),
        cost_estimate=cost(1),
    )(x)


def step_kernel(low_ref, got_ref, level_ref, out_low_ref, out_high_ref, out_level_ref):
    count = low_ref.shape[0]
    half = count // 2
    out_low_ref[...] = low_ref[0:half] + got_ref[0:half]
    out_high_ref[0:half] = low_ref[half:count] + got_ref[half:count]
    level = level_ref[...] + got_ref[count:]
    out_level_ref[...] = level
    out_high_ref[half:] = level


def step(low, got, level):
    half, width = low.shape[0] // 2, low.shape[2]
    counts = (half, half + 1, 1)
    return pl.pallas_call(
        step_kernel,
        out_shape=[jax.ShapeDtypeStruct((n, 2, width), F32) for n in counts],
        compiler_params=params(),
        cost_estimate=cost(1),
    )(low, got, level)


def final_kernel(
    one_ref, far_ref, got_ref, dk_ref, dv_ref, dk2_ref, dv2_ref, out_dk_ref, out_dv_ref
):
    lower = pl.program_id(0) < pl.num_programs(0) // 2
    total = one_ref[...] / POOL1
    triples = (dk_ref, dk2_ref, out_dk_ref), (dv_ref, dv2_ref, out_dv_ref)
    for n, (ref, ref2, out) in enumerate(triples):
        far = far_ref[0, n : n + 1, :] + got_ref[0, n : n + 1, :]
        rows = total[8 * n : 8 * n + 8] + far / POOL2
        for r in range(8):
            at = slice(r * POOL1, (r + 1) * POOL1)
            near = jnp.where(lower, ref[at], ref2[at])
            out[at] = (near + rows[r : r + 1]).astype(BF)


def final(one, far, got, *nears):
    rows, width = nears[0].shape[0], one.shape[1]
    block = 512
    steps = width // block
    whole = pl.BlockSpec((rows, block), lambda i: (0, i))
    return pl.pallas_call(
        final_kernel,
        grid=(steps,),
        in_specs=[
            pl.BlockSpec((16, block), lambda i: (0, i)),
            pl.BlockSpec((1, 2, block), lambda i: (0, 0, i)),
            pl.BlockSpec((2, 2, block), lambda i: (0, 0, i)),
        ]
        + [pl.BlockSpec((rows, block), lambda i: (0, lax.rem(i, steps // 2)))] * 4,
        out_specs=[whole] * 2,
        out_shape=[jax.ShapeDtypeStruct((rows, width), BF)] * 2,
        compiler_params=params(),
        cost_estimate=cost(2),
    )(one, far, got, *nears)


def body(queries, key_rows, values, cotangent, level_bias):
    q, k, v, c = queries[0], key_rows[0], values[0], cotangent[0]
    heads = level_bias.shape[1]
    size = lax.axis_size("seq")
    me = lax.axis_index("seq")
    core = me % 2
    ids = jnp.stack([me, core, size]).astype(jnp.int32)

    kv, qc, *sends = prepare(ids, k, v, q, c)
    x = cross(kv)
    one, far = pool(k, v)
    far = jnp.concatenate([far, swap(far, Z1)], axis=0)
    far = jnp.concatenate([far, swap(far, YA)], axis=0)
    rows = level_rows(one, far, swap(far, YB))

    sk, sv, sq, sc = [swap(s, SIB) for s in sends]
    rows, x, sk, sv, sq, sc = lax.optimization_barrier((rows, x, sk, sv, sq, sc))
    rows = in_group(rows)
    sx = swap(other_half(ids, x), SIB)
    late, rows, sx = lax.optimization_barrier((qc, rows, sx))
    x_qc = cross(late)

    att, satt, dq, sdq, dk, dv, sdk, sdv, grads, stat, sstat = attend(
        ids, level_bias, (q, k, v, c), (sq, sk, sv, sc), x, sx, rows
    )

    rstat = swap(sstat, SIB)
    grads, x_qc, rstat = lax.optimization_barrier((grads, x_qc, rstat))
    grads = in_group(grads)

    stats = jnp.where(core == 0, jnp.stack([stat, rstat]), jnp.stack([rstat, stat]))
    x_stats = cross(stats)
    grads, x_stats = lax.optimization_barrier((grads, x_stats))
    ratt, rdq, rdk, rdv = [swap(s, SIB) for s in (satt, sdq, sdk, sdv)]
    att, dq = join(ids, att, ratt, dq, rdq)
    grads, att, dq = lax.optimization_barrier((grads, att, dq))
    first, second = [
        edge(half, ids, level_bias, k, v, x_qc, x_stats, (dk, rdk, dv, rdv))
        for half in range(2)
    ]

    one, low, high, level = sums(grads)
    low, high, level = step(low, swap(high, YB), level)
    high, first = lax.optimization_barrier((high, first))
    low, high, level = step(low, swap(high, YA), level)
    high, second = lax.optimization_barrier((high, second))
    got = swap(high, Z1)
    dk, dv = final(one, low, got, *first, *second)
    level = level + got[1:]
    level = level + lax.ppermute(level, "batch", [(0, 1), (1, 0)])
    level = level[0, 0].reshape(heads, HEAD)[:, :9].reshape(heads, 3, 3).sum(1).T
    return att[None], dq[None], dk[None], dv[None], level


def solution(mesh):
    rows = P("batch", "seq", None)
    return jax.shard_map(
        body,
        mesh=mesh,
        in_specs=(rows, rows, rows, rows, P()),
        out_specs=(rows, rows, rows, rows, P()),
        check_vma=False,
    )
```
